256 devices in a mesh: row: 8 (over y_lo, x), col: 32 (over y_hi, z, core).
Axes of the slice: x: 4, y: 4 (y_hi: 2, y_lo: 2; y = y_hi * 2 + y_lo), z: 8, core: 2. Of those that a mesh axis runs over, the one named last changes fastest.
Arguments:
- gradient: bfloat16 [16384, 32768], P('row', 'col'), may hold values from -6 to 6
- in_panels: bfloat16 [3, 32768, 256], P(None, 'col'), may hold values from -0.03125 to 0.03125
- out_pool: bfloat16 [32, 16384, 256], P('col', 'row'), may hold values from -0.046875 to 0.046875
- eigenvalues: float32 [3, 256, 256], replicated, may hold values from 0.003 to 0.3
- owners: int32 [3], replicated, may hold values from 0 to 31, as said below
Outputs:
- preconditioned: bfloat16 [16384, 32768], P('row', 'col')
The draws below stay inside these ranges and needn't reach their ends.
Inputs may be any that keep to these rules, and one draw needn't show every extreme that they name: `owners`: each entry names a column group; the last group is named in every draw; entries may repeat.
All inputs are finite; a program needn't handle non-finite values.
Results may differ from the reference program's by a relative error of at most 0.006.
Values may be sent and summed in bfloat16 or wider, within the bound.
No kernel may reach another device: no remote copies, remote signals or barrier semaphores. Data moves between devices by JAX's collectives and lax.ppermute only.
A program may use at most 128 MiB of HBM per device.

```python
import math
import jax
import jax.numpy as jnp
from jax import lax

M = 16384
N = 32768
VEC = 256
NPAN = 3
POOL = 32


def draw_owners(key, part):
    key = jax.random.fold_in(key, 7)
    first, second = jax.random.split(key)
    picks = jax.random.randint(first, (NPAN,), 0, POOL)
    where = jax.random.randint(second, (), 0, NPAN)
    return picks.at[where].set(POOL - 1).astype(jnp.int32)


def level_of(rng, dims, cuts, smallest, top_value):
    level = 1.0
    for dim, shards_of in cuts:
        heights = jax.random.uniform(jax.random.fold_in(jax.random.fold_in(rng, 6), dim), (shards_of,), jnp.float32, smallest / len(cuts), top_value / len(cuts))
        level = level * jnp.repeat(jnp.exp(heights), dims[dim] // shards_of).reshape((-1,) + (1,) * (len(dims) - 1 - dim))
    return level


def scatter_about(own_key, extent, scale, bound, cuts=(), kind=jnp.bfloat16):
    result = scale * jax.random.normal(own_key, extent, jnp.float32)
    if cuts:
        result = result * level_of(own_key, extent, cuts, -0.22, 0.18)
    return jnp.clip(result, -bound, bound).astype(kind)


def setup_inputs(seed: int = 0) -> dict:
    keys = jax.random.split(jax.random.key(seed), 6)
    gradient = scatter_about(keys[0], (M, N), 1.0, 6.0, ((0, 8), (1, 32)))
    in_panels = scatter_about(keys[1], (NPAN, N, VEC), N ** -0.5, 0.03125, ((1, 32),))
    out_pool = scatter_about(keys[2], (POOL, M, VEC), M ** -0.5, 0.046875, ((0, 32), (1, 8)))
    eigenvalues = jnp.clip(jnp.exp(jax.random.uniform(keys[3], (NPAN, VEC, VEC), jnp.float32, math.log(0.003), math.log(0.3))), 0.003, 0.3)
    owners = draw_owners(jax.random.fold_in(keys[5], 71), 0)
    return dict(gradient=gradient, in_panels=in_panels, out_pool=out_pool, eigenvalues=eigenvalues, owners=owners)


def reference(gradient, in_panels, out_pool, eigenvalues, owners):
    total = jnp.zeros((M, N), jnp.float32)
    for number in range(NPAN):
        fetched = out_pool[owners[number]]
        basis = in_panels[number]
        projected = jnp.dot(gradient, basis, preferred_element_type=jnp.float32)
        coupling = jnp.dot(fetched.astype(jnp.float32).T, projected, precision=lax.Precision.HIGHEST, preferred_element_type=jnp.float32)
        values = eigenvalues[number]
        damping = 0.1 * jnp.mean(values)
        scaled = (coupling / (values + damping)).astype(jnp.bfloat16)
        rotated = jnp.dot(fetched, scaled, preferred_element_type=jnp.float32).astype(jnp.bfloat16)
        total = total + jnp.dot(rotated, basis.T, preferred_element_type=jnp.float32)
    return total.astype(jnp.bfloat16)
```

```python
import jax
import jax.numpy as jnp
from jax import lax
from jax.sharding import Mesh
from jax.sharding import PartitionSpec as P

ROW = ("yl", "x")
COL = ("yh", "z", "core")
SPREAD = ("core", "yh", "z")
F32 = jnp.float32
BF16 = jnp.bfloat16


def swap(x, axis):
    return lax.ppermute(x, axis, [(0, 1), (1, 0)])


def paired(x, axis, dim):
    other = swap(x, axis)
    first = lax.axis_index(axis) == 0
    return jnp.concatenate([jnp.where(first, x, other), jnp.where(first, other, x)], axis=dim)


def halved(x, axis):
    here = lax.axis_index(axis)
    half = x.shape[0] // 2
    other = swap(lax.dynamic_slice_in_dim(x, (1 - here) * half, half, 0), axis)
    return lax.dynamic_slice_in_dim(x, here * half, half, 0) + other


def ring(x, axis, size):
    here = lax.axis_index(axis)
    whole = jnp.zeros((size,) + x.shape, x.dtype)
    whole = lax.dynamic_update_index_in_dim(whole, x, here, 0)
    up = down = x
    for step in range(1, size // 2 + 1):
        up = lax.ppermute(up, axis, [(i, (i + 1) % size) for i in range(size)])
        whole = lax.dynamic_update_index_in_dim(whole, up, (here - step) % size, 0)
        if step < size - step:
            down = lax.ppermute(down, axis, [(i, (i - 1) % size) for i in range(size)])
            whole = lax.dynamic_update_index_in_dim(whole, down, (here + step) % size, 0)
    return whole


def everyones(x, axes, count):
    return lax.all_to_all(jnp.broadcast_to(x[None], (count,) + x.shape), axes, 0, 0, tiled=False)


def body(gradient, in_panels, out_pool, eigenvalues, owners):
    count = in_panels.shape[0]
    rows, vec = out_pool.shape[1:]

    with jax.named_scope("panels"):
        pieces = lax.all_to_all(out_pool[0].reshape(32, rows // 32, vec), SPREAD, 0, 0, tiled=False)
        where = (owners % 2) * 16 + owners // 2
        mine = jnp.stack([lax.dynamic_index_in_dim(pieces, where[k], 0, keepdims=False) for k in range(count)])
        both = paired(mine[None], "yh", 0)
        gathered = ring(both, "z", 8)
        half = gathered.transpose(2, 1, 0, 3, 4).reshape(count, rows // 2, vec)
        fetched = paired(half, "core", 1)

    with jax.named_scope("projection"):
        parts = []
        for k in range(count):
            projected = jnp.dot(gradient, in_panels[k], preferred_element_type=F32)
            high = lax.reduce_precision(projected, 8, 7)
            low = (projected - high).astype(BF16)
            split = jnp.concatenate([high.astype(BF16), low], axis=1)
            part = jnp.dot(fetched[k].T, split, preferred_element_type=F32)
            parts.append(part[:, :vec] + part[:, vec:])
        part = jnp.concatenate(parts, axis=0)

    with jax.named_scope("sum"):
        damping = 0.1 * jnp.mean(eigenvalues, axis=(1, 2), keepdims=True)
        below = (eigenvalues + damping).reshape(count * vec, vec)
        part = halved(part, "core")
        exchanged = lax.all_to_all(part.reshape(8, part.shape[0] // 8, vec), ROW, 0, 0, tiled=False)
        part = jnp.sum(exchanged, axis=0)
        part = halved(part, "yh")
        total = jnp.sum(everyones(part, "z", 8), axis=0)
        size = total.shape[0]
        at = (lax.axis_index("core") * 8 + lax.axis_index(ROW)) * 2 + lax.axis_index("yh")
        scaled = (total / lax.dynamic_slice_in_dim(below, at * size, size, 0)).astype(BF16)
        scaled = everyones(scaled, ("core",) + ROW + ("yh",), 32).reshape(count, vec, vec)

    with jax.named_scope("output"):
        out = jnp.zeros(gradient.shape, F32)
        for k in range(count):
            rotated = jnp.dot(fetched[k], scaled[k], preferred_element_type=F32).astype(BF16)
            out = out + lax.dot_general(rotated, in_panels[k], (((1,), (1,)), ((), ())), preferred_element_type=F32)
        return out.astype(BF16)


def solution(mesh):
    fine = Mesh(mesh.devices.reshape(2, 4, 2, 8, 2), ROW + COL)
    return jax.shard_map(
        body,
        mesh=fine,
        in_specs=(P(ROW, COL), P(None, COL, None), P(COL, ROW, None), P(), P()),
        out_specs=P(ROW, COL),
        check_vma=False,
    )
```

```python
import functools

import jax
import jax.numpy as jnp
from jax import lax
from jax.experimental import pallas as pl
from jax.experimental.pallas import tpu as pltpu
from jax.sharding import Mesh
from jax.sharding import PartitionSpec as P

ROW = ("yl", "x")
COL = ("yh", "z", "core")
F32 = jnp.float32
BF16 = jnp.bfloat16
RING = 8
BLOCK = 256
LIMIT = 40 * 1024 * 1024


def swap(x, axis):
    return lax.ppermute(x, axis, [(0, 1), (1, 0)])


def shift(x, by):
    return lax.ppermute(x, "z", [(i, (i + by) % RING) for i in range(RING)])


def params():
    return pltpu.CompilerParams(vmem_limit_bytes=LIMIT)


def call(kernel, grid, in_specs, out_specs, out_shape, flops, moved):
    spec = pltpu.PrefetchScalarGridSpec(num_scalar_prefetch=1, grid=grid, in_specs=in_specs, out_specs=out_specs)
    return pl.pallas_call(
        kernel,
        grid_spec=spec,
        out_shape=out_shape,
        compiler_params=params(),
        cost_estimate=pl.CostEstimate(flops=flops, bytes_accessed=moved, transcendentals=0),
    )


def project_kernel(at_ref, gradient_ref, panels_ref, out_ref):
    for k in range(panels_ref.shape[0]):
        out_ref[k] = jnp.dot(gradient_ref[...], panels_ref[k], preferred_element_type=F32)


def project(gradient, panels, half):
    count, width, vec = panels.shape
    rows = gradient.shape[0] // 2
    steps = rows // BLOCK
    return call(
        project_kernel,
        (steps,),
        [
            pl.BlockSpec((BLOCK, width), lambda i, at: (at[0] * steps + i, 0)),
            pl.BlockSpec((count, width, vec), lambda i, at: (0, 0, 0)),
        ],
        pl.BlockSpec((count, BLOCK, vec), lambda i, at: (0, i, 0)),
        jax.ShapeDtypeStruct((count, rows, vec), F32),
        2 * rows * width * vec * count,
        2 * rows * width + 2 * count * width * vec + 4 * count * rows * vec,
    )(half[None], gradient, panels)


def split_kernel(own_ref, other_ref, out_ref):
    vec = own_ref.shape[2]
    total = (own_ref[0] + other_ref[0]).T
    high = total.astype(BF16)
    out_ref[0, :vec] = high
    out_ref[0, vec:] = (total - high.astype(F32)).astype(BF16)


def split(own, other):
    count, rows, vec = own.shape
    return pl.pallas_call(
        split_kernel,
        grid=(count,),
        in_specs=[pl.BlockSpec((1, rows, vec), lambda k: (k, 0, 0))] * 2,
        out_specs=pl.BlockSpec((1, 2 * vec, rows), lambda k: (k, 0, 0)),
        out_shape=jax.ShapeDtypeStruct((count, 2 * vec, rows), BF16),
        compiler_params=params(),
        cost_estimate=pl.CostEstimate(flops=3 * own.size, bytes_accessed=12 * own.size, transcendentals=0),
    )(own, other)


def couple_kernel(at_ref, terms_ref, fetched_ref, keep_ref, send_ref, total_ref):
    count, rows, vec = fetched_ref.shape
    for k in range(count):
        both = jnp.dot(terms_ref[k], fetched_ref[k], preferred_element_type=F32)
        total_ref[k * vec : (k + 1) * vec] = both[:vec] + both[vec:]
    size = keep_ref.shape[0]
    at = pl.multiple_of(at_ref[0] * size, size)
    other = pl.multiple_of((1 - at_ref[0]) * size, size)
    keep_ref[...] = total_ref[pl.ds(at, size)]
    send_ref[...] = total_ref[pl.ds(other, size)]


def couple(terms, fetched, here):
    count, rows, vec = fetched.shape
    size = count * vec // 2
    half = jax.ShapeDtypeStruct((size, vec), F32)
    whole = pl.BlockSpec(memory_space=pltpu.VMEM)
    return pl.pallas_call(
        couple_kernel,
        in_specs=[pl.BlockSpec(memory_space=pltpu.SMEM), whole, whole],
        out_specs=[whole, whole],
        out_shape=[half, half],
        scratch_shapes=[pltpu.VMEM((count * vec, vec), F32)],
        compiler_params=params(),
        cost_estimate=pl.CostEstimate(flops=4 * fetched.size * vec, bytes_accessed=8 * fetched.size, transcendentals=0),
    )(here[None], terms, fetched)


def apply_kernel(steps, at_ref, own_ref, other_ref, scaled_ref, panels_ref, out_ref):
    def run(fetched_ref):
        total = None
        for k in range(panels_ref.shape[0]):
            rotated = lax.dot_general(fetched_ref[k], scaled_ref[k], (((1,), (1,)), ((), ())), preferred_element_type=F32)
            term = lax.dot_general(rotated.astype(BF16), panels_ref[k], (((1,), (1,)), ((), ())), preferred_element_type=F32)
            total = term if total is None else total + term
        out_ref[...] = total.astype(BF16)

    own = pl.program_id(0) < steps
    pl.when(own)(lambda: run(own_ref))
    pl.when(jnp.logical_not(own))(lambda: run(other_ref))


def apply(own, other, scaled, panels, here):
    count, rows, vec = own.shape
    width = panels.shape[1]
    steps = rows // BLOCK
    return call(
        functools.partial(apply_kernel, steps),
        (2 * steps,),
        [
            pl.BlockSpec((count, BLOCK, vec), lambda i, at: (0, jnp.minimum(i, steps - 1), 0)),
            pl.BlockSpec((count, BLOCK, vec), lambda i, at: (0, jnp.maximum(i - steps, 0), 0)),
            pl.BlockSpec((count, vec, vec), lambda i, at: (0, 0, 0)),
            pl.BlockSpec((count, width, vec), lambda i, at: (0, 0, 0)),
        ],
        pl.BlockSpec((BLOCK, width), lambda i, at: (jnp.where(i < steps, at[0] * steps + i, (1 - at[0]) * steps + i - steps), 0)),
        jax.ShapeDtypeStruct((2 * rows, width), BF16),
        4 * count * rows * vec * (vec + width),
        4 * rows * width + 4 * count * rows * vec,
    )(here[None], own, other, scaled, panels)


def ring(x):
    here = lax.axis_index("z")
    whole = jnp.zeros(x.shape[:1] + (RING,) + x.shape[1:], x.dtype)
    whole = lax.dynamic_update_index_in_dim(whole, x, here, 1)
    up = down = x
    for step in range(1, RING // 2 + 1):
        up = shift(up, 1)
        whole = lax.dynamic_update_index_in_dim(whole, up, (here + RING - step) % RING, 1)
        if step < RING - step:
            down = shift(down, -1)
            whole = lax.dynamic_update_index_in_dim(whole, down, (here + step) % RING, 1)
    return whole


def fetch(panel, owners):
    core, high, here = (lax.axis_index(a) for a in ("core", "yh", "z"))
    rows, vec = panel.shape
    half = rows // 2
    own = lax.dynamic_slice_in_dim(panel, core * half, half, 0)
    other = swap(lax.dynamic_slice_in_dim(panel, (1 - core) * half, half, 0), "core")
    owners = owners[:, None, None]
    of_core, of_ring, of_high = owners % 2, owners // 2 % RING, owners // (2 * RING)
    slots = jnp.where((of_core == core)[..., None], own.reshape(1, RING, half // RING, vec), other.reshape(1, RING, half // RING, vec))
    owned = of_ring == here

    def piece(index):
        return lax.dynamic_index_in_dim(slots, (index + RING) % RING, 1, keepdims=False)

    reach = RING // 2
    up, down = piece(here + reach - 1), piece(here - reach)
    for step in range(1, reach + 1):
        down = jnp.where(owned, piece(here - reach + step), shift(down, -1))
        if step < reach:
            up = jnp.where(owned, piece(here + reach - 1 - step), shift(up, 1))
    mine = jnp.where((here - of_ring + RING) % RING < reach, up, down)
    mine = jnp.where(of_high == high, mine, swap(mine, "yh"))
    return ring(mine).reshape(owners.shape[0], half, vec)


def body(gradient, in_panels, out_pool, eigenvalues, owners):
    core = lax.axis_index("core")
    count, _, vec = in_panels.shape

    with jax.named_scope("panels"):
        own = fetch(out_pool[0], owners)
        other = swap(own, "core")

    with jax.named_scope("projection"):
        sent = swap(project(gradient, in_panels, 1 - core), "core")
        terms = split(project(gradient, in_panels, core), sent)

    with jax.named_scope("coupling"):
        damping = 0.1 * jnp.mean(eigenvalues, axis=(1, 2), keepdims=True)
        below = jnp.swapaxes(eigenvalues + damping, 1, 2).reshape(count * vec, vec)
        keep, send = couple(terms, own, core)
        part = keep + swap(send, "core")
        part = jnp.sum(lax.all_to_all(part.reshape(8, -1, vec), ROW, 0, 0), axis=0)
        copies = jnp.broadcast_to(part.reshape(2, 1, -1, vec), (2, RING, part.shape[0] // 2, vec))
        total = jnp.sum(lax.all_to_all(copies.reshape(2 * RING, -1, vec), ("yh", "z"), 0, 0), axis=0)
        size = total.shape[0]
        at = (core * 8 + lax.axis_index(ROW)) * 2 + lax.axis_index("yh")
        scaled = (total / lax.dynamic_slice_in_dim(below, at * size, size, 0)).astype(BF16)
        copies = jnp.broadcast_to(scaled[None], (32,) + scaled.shape)
        scaled = lax.all_to_all(copies, ("core",) + ROW + ("yh",), 0, 0).reshape(count, vec, vec)

    with jax.named_scope("output"):
        return apply(own, other, scaled, in_panels, core)


def solution(mesh):
    fine = Mesh(mesh.devices.reshape(2, 4, 2, 8, 2), ROW + COL)
    return jax.shard_map(
        body,
        mesh=fine,
        in_specs=(P(ROW, COL), P(None, COL, None), P(COL, ROW, None), P(), P()),
        out_specs=P(ROW, COL),
        check_vma=False,
    )
```

```python
import jax
import jax.numpy as jnp
from jax import lax
from jax.experimental import pallas as pl
from jax.experimental.pallas import tpu as pltpu
from jax.sharding import Mesh
from jax.sharding import PartitionSpec as P

ROW = ("yl", "x")
COL = ("yh", "z", "core")
F32 = jnp.float32
BF16 = jnp.bfloat16
RING = 8
REACH = RING // 2
MIB = 1024 * 1024

VMEM = pl.BlockSpec(memory_space=pltpu.VMEM)
SMEM = pl.BlockSpec(memory_space=pltpu.SMEM)
HBM = pl.BlockSpec(memory_space=pltpu.HBM)
ANY = pl.BlockSpec(memory_space=pl.ANY)


def swap(x, axis):
    return lax.ppermute(x, axis, [(0, 1), (1, 0)])


def shift(x, by):
    return lax.ppermute(x, "z", [(i, (i + by) % RING) for i in range(RING)])


def call(kernel, args, in_specs, out_specs, out_shape, flops=0, scratch=(), limit=16):
    moved = sum(a.size * a.dtype.itemsize for a in args)
    return pl.pallas_call(
        kernel,
        in_specs=in_specs,
        out_specs=out_specs,
        out_shape=out_shape,
        scratch_shapes=scratch,
        compiler_params=pltpu.CompilerParams(vmem_limit_bytes=limit * MIB),
        cost_estimate=pl.CostEstimate(flops=flops, bytes_accessed=moved, transcendentals=0),
    )(*args)


def owner_of(at_ref, k):
    number = at_ref[3 + k]
    return number & 1, (number >> 1) & (RING - 1), number >> 4


def picked(at_ref, k, own_ref, other_ref, index, put):
    core, _, _ = owner_of(at_ref, k)
    rows = own_ref.shape[0] // RING
    span = pl.ds(pl.multiple_of((index & (RING - 1)) * rows, rows), rows)
    pl.when(core == at_ref[0])(lambda: put(own_ref[span]))
    pl.when(core != at_ref[0])(lambda: put(other_ref[span]))


def start_kernel(at_ref, own_ref, other_ref, up_ref, down_ref):
    here = at_ref[2]
    for k in range(up_ref.shape[0]):
        picked(at_ref, k, own_ref, other_ref, here + REACH - 1, lambda x, k=k: up_ref.__setitem__(k, x))
        picked(at_ref, k, own_ref, other_ref, here - REACH + RING, lambda x, k=k: down_ref.__setitem__(k, x))


def merge_kernel(step, at_ref, own_ref, other_ref, came_up_ref, came_down_ref, *refs):
    up_ref, down_ref = refs[-2:]
    here = at_ref[2]
    for k in range(up_ref.shape[0]):
        _, place, _ = owner_of(at_ref, k)

        @pl.when(place == here)
        def _():
            picked(at_ref, k, own_ref, other_ref, here + REACH - 1 - step, lambda x: up_ref.__setitem__(k, x))
            picked(at_ref, k, own_ref, other_ref, here - REACH + RING + step, lambda x: down_ref.__setitem__(k, x))

        @pl.when(place != here)
        def _():
            up_ref[k] = came_up_ref[k]
            down_ref[k] = came_down_ref[k]


def last_kernel(at_ref, own_ref, other_ref, up_ref, came_down_ref, out_ref):
    here = at_ref[2]
    for k in range(out_ref.shape[0]):
        _, place, _ = owner_of(at_ref, k)
        below = ((here - place) & (RING - 1)) < REACH

        @pl.when(below)
        def _():
            out_ref[k] = up_ref[k]

        @pl.when(jnp.logical_not(below))
        def _():
            out_ref[k] = came_down_ref[k]


def level_kernel(at_ref, mine_ref, other_ref, *refs):
    out_ref = refs[-1]
    for k in range(out_ref.shape[0]):
        _, _, high = owner_of(at_ref, k)

        @pl.when(high == at_ref[1])
        def _():
            out_ref[k] = mine_ref[k]

        @pl.when(high != at_ref[1])
        def _():
            out_ref[k] = other_ref[k]


def project_kernel(at_ref, gradient_ref, panels_ref, *refs):
    out_ref, rows_ref, sems = refs[-3:]
    blocks, size, _ = rows_ref.shape
    first = at_ref[0] * (blocks * size)
    copies = []
    for i in range(blocks):
        start = pl.multiple_of(first + i * size, size)
        copies.append(pltpu.make_async_copy(gradient_ref.at[pl.ds(start, size)], rows_ref.at[i], sems.at[i]))
        copies[-1].start()
    for i in range(blocks):
        copies[i].wait()
        for k in range(panels_ref.shape[0]):
            out_ref[k, i * size : (i + 1) * size] = jnp.dot(rows_ref[i], panels_ref[k], preferred_element_type=F32)


def project(gradient, panels, half, after):
    count, width, vec = panels.shape
    rows = gradient.shape[0] // 2
    blocks = 4
    return call(
        project_kernel,
        (half[None], gradient, panels, after),
        [SMEM, HBM, VMEM, ANY],
        VMEM,
        jax.ShapeDtypeStruct((count, rows, vec), F32),
        2 * rows * width * vec * count,
        [pltpu.VMEM((blocks, rows // blocks, width), BF16), pltpu.SemaphoreType.DMA((blocks,))],
    )


def split_kernel(own_ref, other_ref, values_ref, out_ref, below_ref):
    vec = own_ref.shape[2]
    total = (own_ref[0] + other_ref[0]).T
    high = total.astype(BF16)
    out_ref[0, :vec] = high
    out_ref[0, vec:] = (total - high.astype(F32)).astype(BF16)
    values = values_ref[0]
    below_ref[...] = (values + 0.1 * jnp.mean(values)).T


def split(own, other, values):
    count, rows, vec = own.shape
    return pl.pallas_call(
        split_kernel,
        grid=(count,),
        in_specs=[pl.BlockSpec((1, rows, vec), lambda k: (k, 0, 0))] * 2 + [pl.BlockSpec((1, vec, vec), lambda k: (k, 0, 0))],
        out_specs=[pl.BlockSpec((1, 2 * vec, rows), lambda k: (k, 0, 0)), pl.BlockSpec((vec, vec), lambda k: (k, 0))],
        out_shape=[jax.ShapeDtypeStruct((count, 2 * vec, rows), BF16), jax.ShapeDtypeStruct((count * vec, vec), F32)],
        compiler_params=pltpu.CompilerParams(vmem_limit_bytes=20 * MIB),
        cost_estimate=pl.CostEstimate(flops=3 * own.size, bytes_accessed=12 * own.size, transcendentals=0),
    )(own, other, values)


def offsets():
    order = [0]
    for step in range(1, REACH + 1):
        order.append(-step)
        if step < REACH:
            order.append(step)
    return order


def couple_kernel(at_ref, terms_ref, *refs):
    pieces, (keep_ref, send_ref, total_ref) = refs[:RING], refs[RING:]
    count, rows, vec = pieces[0].shape
    for k in range(count):
        both = None
        for piece, offset in zip(pieces, offsets()):
            at = pl.multiple_of(((at_ref[2] + offset + RING) & (RING - 1)) * rows, rows)
            term = jnp.dot(terms_ref[k, :, pl.ds(at, rows)], piece[k], preferred_element_type=F32)
            both = term if both is None else both + term
        total_ref[k * vec : (k + 1) * vec] = both[:vec] + both[vec:]
    size = keep_ref.shape[0]
    keep_ref[...] = total_ref[pl.ds(pl.multiple_of(at_ref[0] * size, size), size)]
    send_ref[...] = total_ref[pl.ds(pl.multiple_of((1 - at_ref[0]) * size, size), size)]


def couple(at, terms, pieces):
    count, rows, vec = pieces[0].shape
    half = jax.ShapeDtypeStruct((count * vec // 2, vec), F32)
    return call(
        couple_kernel,
        (at, terms, *pieces),
        [SMEM] + [VMEM] * (1 + RING),
        [VMEM, VMEM],
        [half, half],
        4 * count * RING * rows * vec * vec,
        [pltpu.VMEM((count * vec, vec), F32)],
    )


def pack_kernel(at_ref, *refs):
    pieces, out_ref = refs[:RING], refs[-1]
    count, rows, _ = pieces[0].shape
    for piece, offset in zip(pieces, offsets()):
        at = pl.multiple_of(((at_ref[2] + offset + RING) & (RING - 1)) * rows, rows)
        for k in range(count):
            out_ref[k, pl.ds(at, rows)] = piece[k]


def pack(at, pieces, after):
    count, rows, vec = pieces[0].shape
    shape = jax.ShapeDtypeStruct((count, RING * rows, vec), BF16)
    return call(pack_kernel, (at, *pieces, after), [SMEM] + [VMEM] * RING + [ANY], VMEM, shape)


def spread_kernel(part_ref, out_ref):
    total = jnp.sum(part_ref[...], axis=0)
    half = total.shape[0] // 2
    for j in range(2 * RING):
        out_ref[j] = total[:half] if j < RING else total[half:]


def spread(parts):
    _, rows, vec = parts.shape
    return call(spread_kernel, (parts,), [VMEM], VMEM, jax.ShapeDtypeStruct((2 * RING, rows // 2, vec), F32))


def scale_kernel(place_ref, parts_ref, below_ref, out_ref):
    total = jnp.sum(parts_ref[...], axis=0)
    size = total.shape[0]
    below = below_ref[pl.ds(pl.multiple_of(place_ref[0] * size, size), size)]
    out_ref[...] = (total / below).astype(BF16)


def apply_kernel(at_ref, own_ref, other_ref, scaled_ref, panels_ref, out_ref, block_ref, sems):
    count, rows, vec = own_ref.shape
    size = block_ref.shape[1]
    steps = rows // size
    core = at_ref[0]
    copies = []
    for number in range(2 * steps):
        fetched_ref, half = (own_ref, core) if number < steps else (other_ref, 1 - core)
        start = (number % steps) * size
        total = None
        for k in range(count):
            rotated = lax.dot_general(fetched_ref[k, start : start + size], scaled_ref[k], (((1,), (1,)), ((), ())), preferred_element_type=F32)
            term = lax.dot_general(rotated.astype(BF16), panels_ref[k], (((1,), (1,)), ((), ())), preferred_element_type=F32)
            total = term if total is None else total + term
        block_ref[number] = total.astype(BF16)
        target = pl.multiple_of(half * rows + start, size)
        copies.append(pltpu.make_async_copy(block_ref.at[number], out_ref.at[pl.ds(target, size)], sems.at[number]))
        copies[-1].start()
    for copy in copies:
        copy.wait()


def apply(at, own, other, scaled, panels):
    count, rows, vec = own.shape
    width = panels.shape[1]
    blocks = 4
    size = 2 * rows // blocks
    return call(
        apply_kernel,
        (at, own, other, scaled, panels),
        [SMEM, VMEM, VMEM, VMEM, VMEM],
        HBM,
        jax.ShapeDtypeStruct((2 * rows, width), BF16),
        4 * count * rows * vec * (vec + width),
        [pltpu.VMEM((blocks, size, width), BF16), pltpu.SemaphoreType.DMA((blocks,))],
        limit=40,
    )


def body(gradient, in_panels, out_pool, eigenvalues, owners):
    core, high, here = (lax.axis_index(a) for a in ("core", "yh", "z"))
    at = jnp.concatenate([jnp.stack([core, high, here]).astype(jnp.int32), owners])
    count, _, vec = in_panels.shape
    panel = out_pool[0]
    half = panel.shape[0] // 2
    piece = jax.ShapeDtypeStruct((count, half // RING, vec), BF16)

    with jax.named_scope("select"):
        own = lax.dynamic_slice_in_dim(panel, core * half, half, 0)
        other = swap(lax.dynamic_slice_in_dim(panel, (1 - core) * half, half, 0), "core")
        up, down = call(start_kernel, (at, own, other), [SMEM, VMEM, VMEM], [VMEM] * 2, [piece] * 2)
        sent = project(gradient, in_panels, 1 - core, up)
        kept = project(gradient, in_panels, core, sent)
        came = swap(sent, "core")
        for step in range(1, REACH):
            after = [(), (sent,), (kept,)][step - 1]
            args = (at, own, other, shift(up, 1), shift(down, -1), *after)

            def kernel(*refs, step=step):
                merge_kernel(step, *refs)

            up, down = call(kernel, args, [SMEM] + [VMEM] * 4 + [ANY] * len(after), [VMEM] * 2, [piece] * 2)
        mine = call(last_kernel, (at, own, other, up, shift(down, -1)), [SMEM] + [VMEM] * 4, VMEM, piece)
        terms, below = split(kept, came, eigenvalues)
        mine = call(level_kernel, (at, mine, swap(mine, "yh"), terms), [SMEM, VMEM, VMEM, ANY], VMEM, piece)

    with jax.named_scope("gather"):
        pieces = [mine]
        up = down = mine
        for step in range(1, REACH + 1):
            up = shift(up, 1)
            pieces.append(up)
            if step < REACH:
                down = shift(down, -1)
                pieces.append(down)

    with jax.named_scope("coupling"):
        keep, send = couple(at, terms, pieces)
        part = keep + swap(send, "core")
        own = pack(at, pieces, part)
        other = swap(own, "core")
        part = spread(lax.all_to_all(part.reshape(8, -1, vec), ROW, 0, 0))
        part = lax.all_to_all(part, ("yh", "z"), 0, 0)
        place = (core * 8 + lax.axis_index(ROW)) * 2 + high
        shape = jax.ShapeDtypeStruct(part.shape[1:], BF16)
        scaled = call(scale_kernel, (place[None], part, below), [SMEM, VMEM, VMEM], VMEM, shape)
        copies = jnp.broadcast_to(scaled[None], (32,) + scaled.shape)
        scaled = lax.all_to_all(copies, ("core",) + ROW + ("yh",), 0, 0).reshape(count, vec, vec)

    with jax.named_scope("output"):
        return apply(at, own, other, scaled, in_panels)


def solution(mesh):
    fine = Mesh(mesh.devices.reshape(2, 4, 2, 8, 2), ROW + COL)
    return jax.shard_map(
        body,
        mesh=fine,
        in_specs=(P(ROW, COL), P(None, COL, None), P(COL, ROW, None), P(), P()),
        out_specs=P(ROW, COL),
        check_vma=False,
    )
```

```python
import functools

import jax
import jax.numpy as jnp
from jax import lax
from jax.experimental import pallas as pl
from jax.experimental.pallas import tpu as pltpu
from jax.sharding import Mesh
from jax.sharding import PartitionSpec as P

ROW = ("yl", "x")
COL = ("yh", "z", "core")
PLANE = ("core", "yl", "x", "yh")
F32 = jnp.float32
BF16 = jnp.bfloat16
RING = 8
REACH = RING // 2
BLOCKS = 4
MIB = 1024 * 1024

VMEM = pl.BlockSpec(memory_space=pltpu.VMEM)
SMEM = pl.BlockSpec(memory_space=pltpu.SMEM)
ANY = pl.BlockSpec(memory_space=pl.ANY)
TOKEN = jax.ShapeDtypeStruct((8, 128), F32)


def swap(x, axis):
    return lax.ppermute(x, axis, [(0, 1), (1, 0)])


def shift(x, by):
    return lax.ppermute(x, "z", [(i, (i + by) % RING) for i in range(RING)])


def call(kernel, args, in_specs, out_specs, out_shape, flops=0, scratch=(), limit=16):
    moved = sum(a.size * a.dtype.itemsize for a in args)
    return pl.pallas_call(
        kernel,
        in_specs=in_specs,
        out_specs=out_specs,
        out_shape=out_shape,
        scratch_shapes=scratch,
        compiler_params=pltpu.CompilerParams(vmem_limit_bytes=limit * MIB),
        cost_estimate=pl.CostEstimate(flops=flops, bytes_accessed=moved, transcendentals=0),
    )(*args)


def owner_of(at_ref, k):
    number = at_ref[4 + k]
    return number & 1, (number >> 1) & (RING - 1), number >> 4


def picked(at_ref, k, own_ref, other_ref, index, put):
    core, _, _ = owner_of(at_ref, k)
    rows = own_ref.shape[0] // RING
    span = pl.ds(pl.multiple_of((index & (RING - 1)) * rows, rows), rows)
    pl.when(core == at_ref[0])(lambda: put(own_ref[span]))
    pl.when(core != at_ref[0])(lambda: put(other_ref[span]))


def start_kernel(at_ref, own_ref, other_ref, up_ref, down_ref, token_ref):
    here = at_ref[2]
    for k in range(up_ref.shape[0]):
        picked(at_ref, k, own_ref, other_ref, here + REACH - 1, lambda x, k=k: up_ref.__setitem__(k, x))
        picked(at_ref, k, own_ref, other_ref, here - REACH + RING, lambda x, k=k: down_ref.__setitem__(k, x))
    token_ref[...] = jnp.zeros_like(token_ref)


def merge_kernel(step, at_ref, own_ref, other_ref, came_up_ref, came_down_ref, _, up_ref, down_ref, token_ref):
    here = at_ref[2]
    for k in range(up_ref.shape[0]):
        _, place, _ = owner_of(at_ref, k)

        @pl.when(place == here)
        def _():
            picked(at_ref, k, own_ref, other_ref, here + REACH - 1 - step, lambda x: up_ref.__setitem__(k, x))
            picked(at_ref, k, own_ref, other_ref, here - REACH + RING + step, lambda x: down_ref.__setitem__(k, x))

        @pl.when(place != here)
        def _():
            up_ref[k] = came_up_ref[k]
            down_ref[k] = came_down_ref[k]

    token_ref[...] = jnp.zeros_like(token_ref)


def last_kernel(at_ref, up_ref, came_down_ref, _, out_ref, token_ref):
    here = at_ref[2]
    for k in range(out_ref.shape[0]):
        _, place, _ = owner_of(at_ref, k)
        below = ((here - place) & (RING - 1)) < REACH

        @pl.when(below)
        def _():
            out_ref[k] = up_ref[k]

        @pl.when(jnp.logical_not(below))
        def _():
            out_ref[k] = came_down_ref[k]

    token_ref[...] = jnp.zeros_like(token_ref)


def level_kernel(at_ref, mine_ref, other_ref, _, out_ref):
    for k in range(out_ref.shape[0]):
        _, _, high = owner_of(at_ref, k)

        @pl.when(high == at_ref[1])
        def _():
            out_ref[k] = mine_ref[k]

        @pl.when(high != at_ref[1])
        def _():
            out_ref[k] = other_ref[k]


def project_kernel(number, _, gradient_ref, panels_ref, out_ref, token_ref, rows_ref, sem):
    size = rows_ref.shape[0]
    vec = panels_ref.shape[2]
    copy = pltpu.make_async_copy(gradient_ref.at[pl.ds(number * size, size)], rows_ref, sem)
    copy.start()
    copy.wait()
    for k in range(panels_ref.shape[0]):
        total = jnp.dot(rows_ref[...], panels_ref[k], preferred_element_type=F32).T
        high = total.astype(BF16)
        out_ref[k, :vec] = high
        out_ref[k, vec:] = (total - high.astype(F32)).astype(BF16)
    token_ref[...] = jnp.zeros_like(token_ref)


def project(number, token, gradient, panels):
    count, width, vec = panels.shape
    size = gradient.shape[0] // BLOCKS
    return call(
        functools.partial(project_kernel, number),
        (token, gradient, panels),
        [ANY, ANY, VMEM],
        [VMEM, VMEM],
        [jax.ShapeDtypeStruct((count, 2 * vec, size), BF16), TOKEN],
        2 * size * width * vec * count,
        [pltpu.VMEM((size, width), BF16), pltpu.SemaphoreType.DMA],
    )


def damp_kernel(at_ref, values_ref, _, out_ref, token_ref, all_ref):
    count, vec, _ = values_ref.shape
    for k in range(count):
        values = values_ref[k]
        all_ref[k * vec : (k + 1) * vec] = (values + 0.1 * jnp.mean(values)).T
    size = out_ref.shape[0]
    out_ref[...] = all_ref[pl.ds(pl.multiple_of(at_ref[3] * size, size), size)]
    token_ref[...] = jnp.zeros_like(token_ref)


def damp(at, values, places, token):
    count, vec, _ = values.shape
    size = count * vec // places
    shapes = [jax.ShapeDtypeStruct((size, vec), F32), TOKEN]
    return call(damp_kernel, (at, values, token), [SMEM, VMEM, ANY], [VMEM, VMEM], shapes, scratch=[pltpu.VMEM((count * vec, vec), F32)])


def offsets():
    order = [0]
    for step in range(1, REACH + 1):
        order.append(-step)
        if step < REACH:
            order.append(step)
    return order


def first_row(at_ref, own, offset, rows):
    half = at_ref[0] if own else 1 - at_ref[0]
    return pl.multiple_of((half * RING + ((at_ref[2] + offset + RING) & (RING - 1))) * rows, rows)


def early_kernel(at_ref, *refs):
    terms, refs = refs[:BLOCKS], refs[BLOCKS:]
    pieces, (total_ref, all_ref) = refs[: 2 * (RING - 1)], refs[2 * (RING - 1) :]
    count, rows, vec = pieces[0].shape
    order = [(own, offset) for offset in offsets()[:-1] for own in (True, False)]
    for piece, (own, offset) in zip(pieces, order):
        span = pl.ds(first_row(at_ref, own, offset, rows), rows)
        for k in range(count):
            all_ref[k, span] = piece[k]
    for own in (True, False):
        span = pl.ds(first_row(at_ref, own, REACH, rows), rows)
        for k in range(count):
            all_ref[k, span] = jnp.zeros((rows, vec), BF16)
    size = all_ref.shape[1] // BLOCKS
    for k in range(count):
        both = None
        for b in range(BLOCKS):
            term = jnp.dot(terms[b][k], all_ref[k, b * size : (b + 1) * size], preferred_element_type=F32)
            both = term if both is None else both + term
        total_ref[k * vec : (k + 1) * vec] = both[:vec] + both[vec:]


def early(at, terms, pieces):
    count, rows, vec = pieces[0].shape
    shapes = [jax.ShapeDtypeStruct((count * vec, vec), F32), jax.ShapeDtypeStruct((count, 2 * RING * rows, vec), BF16)]
    specs = [SMEM] + [VMEM] * (BLOCKS + len(pieces))
    return call(early_kernel, (at, *terms, *pieces), specs, [VMEM, VMEM], shapes, 4 * count * RING * rows * vec * vec)


def late_kernel(at_ref, *refs):
    terms, (total_ref, own_ref, other_ref, out_ref) = refs[:BLOCKS], refs[BLOCKS:]
    count, rows, vec = own_ref.shape
    size = terms[0].shape[2]
    out_ref[...] = total_ref[...]
    for own, piece in ((True, own_ref), (False, other_ref)):
        first = first_row(at_ref, own, REACH, rows)
        for b in range(BLOCKS):

            @pl.when(first // size == b)
            def _():
                span = pl.ds(pl.multiple_of(first - b * size, rows), rows)
                for k in range(count):
                    both = jnp.dot(terms[b][k, :, span], piece[k], preferred_element_type=F32)
                    out_ref[k * vec : (k + 1) * vec] += both[:vec] + both[vec:]


def late(at, terms, total, own, other):
    specs = [SMEM] + [VMEM] * (BLOCKS + 3)
    return call(late_kernel, (at, *terms, total, own, other), specs, VMEM, jax.ShapeDtypeStruct(total.shape, F32))


def spread_kernel(part_ref, out_ref):
    total = jnp.sum(part_ref[...], axis=0)
    for j in range(RING):
        out_ref[j] = total


def spread(parts):
    return call(spread_kernel, (parts,), [VMEM], VMEM, jax.ShapeDtypeStruct((RING,) + parts.shape[1:], F32))


def scale_kernel(parts_ref, below_ref, out_ref):
    out_ref[...] = (jnp.sum(parts_ref[...], axis=0) / below_ref[...]).astype(BF16)


def apply_kernel(at_ref, own_ref, other_ref, all_ref, scaled_ref, panels_ref, out_ref, fetched_ref, block_ref, in_sem, sems):
    steps, size, _ = block_ref.shape
    count, rows, _ = own_ref.shape
    fetch = pltpu.make_async_copy(all_ref, fetched_ref, in_sem)
    fetch.start()
    fetch.wait()
    for own, piece in ((True, own_ref), (False, other_ref)):
        span = pl.ds(first_row(at_ref, own, REACH, rows), rows)
        for k in range(count):
            fetched_ref[k, span] = piece[k]
    copies = []
    for number in range(steps):
        total = None
        span = slice(number * size, (number + 1) * size)
        for k in range(count):
            rotated = lax.dot_general(fetched_ref[k, span], scaled_ref[k], (((1,), (1,)), ((), ())), preferred_element_type=F32)
            term = lax.dot_general(rotated.astype(BF16), panels_ref[k], (((1,), (1,)), ((), ())), preferred_element_type=F32)
            total = term if total is None else total + term
        block_ref[number] = total.astype(BF16)
        copies.append(pltpu.make_async_copy(block_ref.at[number], out_ref.at[pl.ds(number * size, size)], sems.at[number]))
        copies[-1].start()
    for copy in copies:
        copy.wait()


def apply(at, own, other, fetched, scaled, panels):
    count, rows, vec = fetched.shape
    width = panels.shape[1]
    steps = 4
    return call(
        apply_kernel,
        (at, own, other, fetched, scaled, panels),
        [SMEM, VMEM, VMEM, ANY, VMEM, VMEM],
        ANY,
        jax.ShapeDtypeStruct((rows, width), BF16),
        2 * count * rows * vec * (vec + width),
        [
            pltpu.VMEM(fetched.shape, BF16),
            pltpu.VMEM((steps, rows // steps, width), BF16),
            pltpu.SemaphoreType.DMA,
            pltpu.SemaphoreType.DMA((steps,)),
        ],
        limit=24,
    )


def body(gradient, in_panels, out_pool, eigenvalues, owners):
    core, high, here = (lax.axis_index(a) for a in ("core", "yh", "z"))
    at = jnp.concatenate([jnp.stack([core, high, here, lax.axis_index(PLANE)]).astype(jnp.int32), owners])
    count, _, vec = in_panels.shape
    panel = out_pool[0]
    half = panel.shape[0] // 2
    piece = jax.ShapeDtypeStruct((count, half // RING, vec), BF16)
    terms = []

    with jax.named_scope("select"):
        own = lax.dynamic_slice_in_dim(panel, core * half, half, 0)
        other = swap(lax.dynamic_slice_in_dim(panel, (1 - core) * half, half, 0), "core")
        up, down, token = call(start_kernel, (at, own, other), [SMEM, VMEM, VMEM], [VMEM] * 3, [piece] * 2 + [TOKEN])
        for step in range(1, REACH):
            term, token = project(step - 1, token, gradient, in_panels)
            terms.append(term)
            args = (at, own, other, shift(up, 1), shift(down, -1), token)
            kernel = functools.partial(merge_kernel, step)
            up, down, token = call(kernel, args, [SMEM] + [VMEM] * 4 + [ANY], [VMEM] * 3, [piece] * 2 + [TOKEN])
        term, token = project(REACH - 1, token, gradient, in_panels)
        terms.append(term)
        mine, token = call(last_kernel, (at, up, shift(down, -1), token), [SMEM] + [VMEM] * 2 + [ANY], [VMEM] * 2, [piece, TOKEN])
        below, token = damp(at, eigenvalues, 32, token)
        mine = call(level_kernel, (at, mine, swap(mine, "yh"), token), [SMEM] + [VMEM] * 2 + [ANY], VMEM, piece)

    with jax.named_scope("gather"):
        pieces = [mine, swap(mine, "core")]
        up = down = mine
        for _ in range(1, REACH):
            up, down = shift(up, 1), shift(down, -1)
            pieces += [up, swap(up, "core"), down, swap(down, "core")]
        pieces += [shift(up, 1), shift(pieces[-1], -1)]

    with jax.named_scope("coupling"):
        part, fetched = early(at, terms, pieces[:-2])
        part = late(at, terms, part, *pieces[-2:])
        part = spread(lax.all_to_all(part.reshape(32, -1, vec), PLANE, 0, 0))
        part = lax.all_to_all(part, "z", 0, 0)
        scaled = call(scale_kernel, (part, below), [VMEM, VMEM], VMEM, jax.ShapeDtypeStruct(part.shape[1:], BF16))
        copies = jnp.broadcast_to(scaled[None], (32,) + scaled.shape)
        scaled = lax.all_to_all(copies, PLANE, 0, 0).reshape(count, vec, vec)

    with jax.named_scope("output"):
        return apply(at, *pieces[-2:], fetched, scaled, in_panels)


def solution(mesh):
    fine = Mesh(mesh.devices.reshape(2, 4, 2, 8, 2), ROW + COL)
    return jax.shard_map(
        body,
        mesh=fine,
        in_specs=(P(ROW, COL), P(None, COL, None), P(COL, ROW, None), P(), P()),
        out_specs=P(ROW, COL),
        check_vma=False,
    )
```

```python
import functools

import jax
import jax.numpy as jnp
from jax import lax
from jax.experimental import pallas as pl
from jax.experimental.pallas import tpu as pltpu
from jax.sharding import Mesh
from jax.sharding import PartitionSpec as P

ROW = ("yl", "x")
COL = ("yh", "z", "core")
SPREAD = ("core", "z", "yh")
PLANE = ("core", "yl", "x", "yh")
F32 = jnp.float32
BF16 = jnp.bfloat16
RING = 8
REACH = RING // 2
BLOCKS = 4
MIB = 1024 * 1024

VMEM = pl.BlockSpec(memory_space=pltpu.VMEM)
SMEM = pl.BlockSpec(memory_space=pltpu.SMEM)
ANY = pl.BlockSpec(memory_space=pl.ANY)
TOKEN = jax.ShapeDtypeStruct((8, 128), F32)


def swap(x, axis):
    return lax.ppermute(x, axis, [(0, 1), (1, 0)])


def shift(x, by):
    return lax.ppermute(x, "z", [(i, (i + by) % RING) for i in range(RING)])


def call(kernel, args, in_specs, out_specs, out_shape, flops=0, scratch=(), limit=16):
    moved = sum(a.size * a.dtype.itemsize for a in args)
    return pl.pallas_call(
        kernel,
        in_specs=in_specs,
        out_specs=out_specs,
        out_shape=out_shape,
        scratch_shapes=scratch,
        compiler_params=pltpu.CompilerParams(vmem_limit_bytes=limit * MIB),
        cost_estimate=pl.CostEstimate(flops=flops, bytes_accessed=moved, transcendentals=0),
    )(*args)


def owner_of(at_ref, k):
    number = at_ref[4 + k]
    return number & 1, (number >> 1) & (RING - 1), number >> 4


def pick_kernel(at_ref, all_ref, _, out_ref, sems):
    copies = []
    for k in range(out_ref.shape[0]):
        core, place, high = owner_of(at_ref, k)
        number = core * (2 * RING) + place * 2 + high
        copies.append(pltpu.make_async_copy(all_ref.at[number], out_ref.at[k], sems.at[k]))
        copies[-1].start()
    for copy in copies:
        copy.wait()


def pair_kernel(at_ref, mine_ref, other_ref, out_ref):
    rows = mine_ref.shape[1]
    mine = pl.ds(pl.multiple_of(at_ref[1] * rows, rows), rows)
    other = pl.ds(pl.multiple_of((1 - at_ref[1]) * rows, rows), rows)
    for k in range(mine_ref.shape[0]):
        out_ref[k, mine] = mine_ref[k]
        out_ref[k, other] = other_ref[k]


def project_kernel(own, at_ref, gradient_ref, panels_ref, out_ref, rows_ref, sems):
    blocks, size, _ = rows_ref.shape
    half = at_ref[0] if own else 1 - at_ref[0]
    copies = []
    for i in range(blocks):
        start = pl.multiple_of((half * blocks + i) * size, size)
        copies.append(pltpu.make_async_copy(gradient_ref.at[pl.ds(start, size)], rows_ref.at[i], sems.at[i]))
        copies[-1].start()
    for i in range(blocks):
        copies[i].wait()
        for k in range(panels_ref.shape[0]):
            out_ref[k, i * size : (i + 1) * size] = jnp.dot(rows_ref[i], panels_ref[k], preferred_element_type=F32)


def project(at, own, gradient, panels):
    count, width, vec = panels.shape
    rows = gradient.shape[0] // 2
    return call(
        functools.partial(project_kernel, own),
        (at, gradient, panels),
        [SMEM, ANY, VMEM],
        VMEM,
        jax.ShapeDtypeStruct((count, rows, vec), F32),
        2 * rows * width * vec * count,
        [pltpu.VMEM((BLOCKS, rows // BLOCKS, width), BF16), pltpu.SemaphoreType.DMA((BLOCKS,))],
        limit=60,
    )


def split_kernel(at_ref, own_ref, other_ref, values_ref, out_ref, below_ref, token_ref, all_ref):
    count, _, vec = own_ref.shape
    for k in range(count):
        total = (own_ref[k] + other_ref[k]).T
        high = total.astype(BF16)
        out_ref[k, :vec] = high
        out_ref[k, vec:] = (total - high.astype(F32)).astype(BF16)
        values = values_ref[k]
        all_ref[k * vec : (k + 1) * vec] = (values + 0.1 * jnp.mean(values)).T
    size = below_ref.shape[0]
    below_ref[...] = all_ref[pl.ds(pl.multiple_of(at_ref[3] * size, size), size)]
    token_ref[...] = jnp.zeros_like(token_ref)


def split(at, own, other, values, places):
    count, rows, vec = own.shape
    shapes = [jax.ShapeDtypeStruct((count, 2 * vec, rows), BF16), jax.ShapeDtypeStruct((count * vec // places, vec), F32), TOKEN]
    return call(split_kernel, (at, own, other, values), [SMEM] + [VMEM] * 3, [VMEM] * 3, shapes, scratch=[pltpu.VMEM((count * vec, vec), F32)])


def offsets():
    order = [0]
    for step in range(1, REACH + 1):
        order.append(-step)
        if step < REACH:
            order.append(step)
    return order


def first_row(at_ref, offset, rows):
    return pl.multiple_of(((at_ref[2] + offset + RING) & (RING - 1)) * rows, rows)


def early_kernel(at_ref, terms_ref, *refs):
    pieces, (total_ref, half_ref) = refs[: RING - 1], refs[RING - 1 :]
    count, rows, vec = pieces[0].shape
    for piece, offset in zip(pieces, offsets()):
        span = pl.ds(first_row(at_ref, offset, rows), rows)
        for k in range(count):
            half_ref[k, span] = piece[k]
    span = pl.ds(first_row(at_ref, REACH, rows), rows)
    for k in range(count):
        half_ref[k, span] = jnp.zeros((rows, vec), BF16)
        both = jnp.dot(terms_ref[k], half_ref[k], preferred_element_type=F32)
        total_ref[k * vec : (k + 1) * vec] = both[:vec] + both[vec:]


def early(at, terms, pieces):
    count, rows, vec = pieces[0].shape
    shapes = [jax.ShapeDtypeStruct((count * vec, vec), F32), jax.ShapeDtypeStruct((count, RING * rows, vec), BF16)]
    specs = [SMEM] + [VMEM] * (1 + len(pieces))
    return call(early_kernel, (at, terms, *pieces), specs, [VMEM, VMEM], shapes, 4 * count * RING * rows * vec * vec)


def late_kernel(at_ref, terms_ref, total_ref, half_ref, piece_ref, out_ref, whole_ref):
    count, rows, vec = piece_ref.shape
    span = pl.ds(first_row(at_ref, REACH, rows), rows)
    for k in range(count):
        both = jnp.dot(terms_ref[k, :, span], piece_ref[k], preferred_element_type=F32)
        panel = slice(k * vec, (k + 1) * vec)
        out_ref[panel] = total_ref[panel] + both[:vec] + both[vec:]
        whole_ref[k] = half_ref[k]
        whole_ref[k, span] = piece_ref[k]


def late(at, terms, total, half, piece):
    shapes = [jax.ShapeDtypeStruct(total.shape, F32), jax.ShapeDtypeStruct(half.shape, BF16)]
    return call(late_kernel, (at, terms, total, half, piece), [SMEM] + [VMEM] * 4, [VMEM, VMEM], shapes)


def spread_kernel(part_ref, out_ref):
    total = jnp.sum(part_ref[...], axis=0)
    for j in range(RING):
        out_ref[j] = total


def spread(parts):
    return call(spread_kernel, (parts,), [VMEM], VMEM, jax.ShapeDtypeStruct((RING,) + parts.shape[1:], F32))


def scale_kernel(parts_ref, below_ref, out_ref):
    out_ref[...] = (jnp.sum(parts_ref[...], axis=0) / below_ref[...]).astype(BF16)


def apply_kernel(at_ref, own_ref, other_ref, scaled_ref, panels_ref, out_ref, fetched_ref, block_ref, in_sems, out_sems):
    steps, size, _ = block_ref.shape
    count, half, _ = own_ref.shape
    near = steps // 2
    fetches, copies = [], []
    for number in range(steps):
        ref = own_ref if number < near else other_ref
        rows = pl.ds((number % near) * size, size)
        fetches.append(pltpu.make_async_copy(ref.at[:, rows], fetched_ref.at[number], in_sems.at[number]))
        fetches[-1].start()
    for number in range(steps):
        fetches[number].wait()
        total = None
        for k in range(count):
            rotated = lax.dot_general(fetched_ref[number, k], scaled_ref[k], (((1,), (1,)), ((), ())), preferred_element_type=F32)
            term = lax.dot_general(rotated.astype(BF16), panels_ref[k], (((1,), (1,)), ((), ())), preferred_element_type=F32)
            total = term if total is None else total + term
        block_ref[number] = total.astype(BF16)
        first = at_ref[0] if number < near else 1 - at_ref[0]
        target = pl.multiple_of(first * half + (number % near) * size, size)
        copies.append(pltpu.make_async_copy(block_ref.at[number], out_ref.at[pl.ds(target, size)], out_sems.at[number]))
        copies[-1].start()
    for copy in copies:
        copy.wait()


def apply(at, own, other, scaled, panels):
    count, rows, vec = other.shape
    width = panels.shape[1]
    steps = 4
    size = 2 * rows // steps
    return call(
        apply_kernel,
        (at, own, other, scaled, panels),
        [SMEM, ANY, ANY, VMEM, VMEM],
        ANY,
        jax.ShapeDtypeStruct((2 * rows, width), BF16),
        4 * count * rows * vec * (vec + width),
        [
            pltpu.VMEM((steps, count, size, vec), BF16),
            pltpu.VMEM((steps, size, width), BF16),
            pltpu.SemaphoreType.DMA((steps,)),
            pltpu.SemaphoreType.DMA((steps,)),
        ],
        limit=24,
    )


def body(gradient, in_panels, out_pool, eigenvalues, owners):
    core, high, here = (lax.axis_index(a) for a in ("core", "yh", "z"))
    at = jnp.concatenate([jnp.stack([core, high, here, lax.axis_index(PLANE)]).astype(jnp.int32), owners])
    count, _, vec = in_panels.shape
    size = out_pool.shape[1] // 32
    piece = jax.ShapeDtypeStruct((count, size, vec), BF16)
    pair = jax.ShapeDtypeStruct((count, 2 * size, vec), BF16)

    with jax.named_scope("scatter"):
        every = lax.all_to_all(out_pool.reshape(32, size, vec), SPREAD, 0, 0)

    with jax.named_scope("projection"):
        came = swap(project(at, False, gradient, in_panels), "core")
        terms, below, token = split(at, project(at, True, gradient, in_panels), came, eigenvalues, 32)

    with jax.named_scope("gather"):
        mine = call(pick_kernel, (at, every, token), [SMEM, ANY, ANY], VMEM, piece, scratch=[pltpu.SemaphoreType.DMA((count,))])
        mine = call(pair_kernel, (at, mine, swap(mine, "yh")), [SMEM, VMEM, VMEM], VMEM, pair)
        pieces = [mine]
        up = down = mine
        for _ in range(1, REACH):
            up, down = shift(up, 1), shift(down, -1)
            pieces += [up, down]
        pieces.append(shift(up, 1))

    with jax.named_scope("coupling"):
        part, own = early(at, terms, pieces[:-1])
        part, own = late(at, terms, part, own, pieces[-1])
        other = swap(own, "core")
        part = spread(lax.all_to_all(part.reshape(32, -1, vec), PLANE, 0, 0))
        part = lax.all_to_all(part, "z", 0, 0)
        scaled = call(scale_kernel, (part, below), [VMEM, VMEM], VMEM, jax.ShapeDtypeStruct(part.shape[1:], BF16))
        copies = jnp.broadcast_to(scaled[None], (32,) + scaled.shape)
        scaled = lax.all_to_all(copies, PLANE, 0, 0).reshape(count, vec, vec)

    with jax.named_scope("output"):
        return apply(at, own, other, scaled, in_panels)


def solution(mesh):
    fine = Mesh(mesh.devices.reshape(2, 4, 2, 8, 2), ROW + COL)
    return jax.shard_map(
        body,
        mesh=fine,
        in_specs=(P(ROW, COL), P(None, COL, None), P(COL, ROW, None), P(), P()),
        out_specs=P(ROW, COL),
        check_vma=False,
    )
```

```python
import functools

import jax
import jax.numpy as jnp
from jax import lax
from jax.experimental import pallas as pl
from jax.experimental.pallas import tpu as pltpu
from jax.sharding import Mesh
from jax.sharding import PartitionSpec as P

ROW = ("yl", "x")
COL = ("yh", "z", "core")
PLANE = ("core", "yl", "x", "yh")
F32 = jnp.float32
BF16 = jnp.bfloat16
RING = 8
REACH = RING // 2
BLOCKS = 4
MIB = 1024 * 1024

VMEM = pl.BlockSpec(memory_space=pltpu.VMEM)
SMEM = pl.BlockSpec(memory_space=pltpu.SMEM)
ANY = pl.BlockSpec(memory_space=pl.ANY)
TOKEN = jax.ShapeDtypeStruct((8, 128), F32)


def swap(x, axis):
    return lax.ppermute(x, axis, [(0, 1), (1, 0)])


def shift(x, by):
    return lax.ppermute(x, "z", [(i, (i + by) % RING) for i in range(RING)])


def call(kernel, args, in_specs, out_specs, out_shape, flops=0, scratch=(), limit=16):
    moved = sum(a.size * a.dtype.itemsize for a in args)
    return pl.pallas_call(
        kernel,
        in_specs=in_specs,
        out_specs=out_specs,
        out_shape=out_shape,
        scratch_shapes=scratch,
        compiler_params=pltpu.CompilerParams(vmem_limit_bytes=limit * MIB),
        cost_estimate=pl.CostEstimate(flops=flops, bytes_accessed=moved, transcendentals=0),
    )(*args)


def owner_of(at_ref, k):
    number = at_ref[4 + k]
    return number & 1, (number >> 1) & (RING - 1), number >> 4


def pick_kernel(at_ref, all_ref, _one, _two, keep_ref, send_ref, sems):
    rows = keep_ref.shape[1]
    copies = []
    for k in range(keep_ref.shape[0]):
        _, place, _ = owner_of(at_ref, k)
        for half, ref in ((at_ref[0], keep_ref), (1 - at_ref[0], send_ref)):
            span = pl.ds(pl.multiple_of(half * rows, rows), rows)
            copies.append(pltpu.make_async_copy(all_ref.at[place, span], ref.at[k], sems.at[len(copies)]))
            copies[-1].start()
    for copy in copies:
        copy.wait()


def level_kernel(axis, at_ref, mine_ref, other_ref, out_ref, token_ref):
    for k in range(out_ref.shape[0]):
        core, _, high = owner_of(at_ref, k)
        mine = (core, high)[axis] == at_ref[axis]

        @pl.when(mine)
        def _():
            out_ref[k] = mine_ref[k]

        @pl.when(jnp.logical_not(mine))
        def _():
            out_ref[k] = other_ref[k]

    token_ref[...] = jnp.zeros_like(token_ref)


def level(axis, at, mine, other):
    return call(functools.partial(level_kernel, axis), (at, mine, other), [SMEM, VMEM, VMEM], [VMEM] * 2, [jax.ShapeDtypeStruct(mine.shape, mine.dtype), TOKEN])


def project_kernel(own, at_ref, gradient_ref, panels_ref, out_ref, token_ref, rows_ref, sems):
    rows = rows_ref.shape[0] // RING
    half = at_ref[0] if own else 1 - at_ref[0]
    copies = []
    for i in range(RING):
        start = pl.multiple_of((2 * i + half) * rows, rows)
        copies.append(pltpu.make_async_copy(gradient_ref.at[pl.ds(start, rows)], rows_ref.at[pl.ds(i * rows, rows)], sems.at[i]))
        copies[-1].start()
    for i in range(0, RING, 2):
        copies[i].wait()
        copies[i + 1].wait()
        span = slice(i * rows, (i + 2) * rows)
        for k in range(panels_ref.shape[0]):
            out_ref[k, span] = jnp.dot(rows_ref[span], panels_ref[k], preferred_element_type=F32)
    token_ref[...] = jnp.zeros_like(token_ref)


def project(at, own, gradient, panels):
    count, width, vec = panels.shape
    rows = gradient.shape[0] // 2
    return call(
        functools.partial(project_kernel, own),
        (at, gradient, panels),
        [SMEM, ANY, VMEM],
        [VMEM, VMEM],
        [jax.ShapeDtypeStruct((count, rows, vec), F32), TOKEN],
        2 * rows * width * vec * count,
        [pltpu.VMEM((rows, width), BF16), pltpu.SemaphoreType.DMA((RING,))],
    )


def split_kernel(at_ref, own_ref, other_ref, values_ref, _, out_ref, below_ref, all_ref):
    count, _, vec = own_ref.shape
    for k in range(count):
        total = (own_ref[k] + other_ref[k]).T
        high = total.astype(BF16)
        out_ref[k, :vec] = high
        out_ref[k, vec:] = (total - high.astype(F32)).astype(BF16)
        values = values_ref[k]
        all_ref[k * vec : (k + 1) * vec] = (values + 0.1 * jnp.mean(values)).T
    size = below_ref.shape[0]
    below_ref[...] = all_ref[pl.ds(pl.multiple_of(at_ref[3] * size, size), size)]


def split(at, own, other, values, places, token):
    count, rows, vec = own.shape
    shapes = [jax.ShapeDtypeStruct((count, 2 * vec, rows), BF16), jax.ShapeDtypeStruct((count * vec // places, vec), F32)]
    return call(split_kernel, (at, own, other, values, token), [SMEM] + [VMEM] * 3 + [ANY], [VMEM] * 2, shapes, scratch=[pltpu.VMEM((count * vec, vec), F32)])


def offsets():
    order = [0]
    for step in range(1, REACH + 1):
        order.append(-step)
        if step < REACH:
            order.append(step)
    return order


def first_row(at_ref, offset, rows):
    return pl.multiple_of(((at_ref[2] + offset + RING) & (RING - 1)) * rows, rows)


def early_kernel(at_ref, terms_ref, *refs):
    pieces, (total_ref, half_ref) = refs[: RING - 1], refs[RING - 1 :]
    count, rows, vec = pieces[0].shape
    for piece, offset in zip(pieces, offsets()):
        span = pl.ds(first_row(at_ref, offset, rows), rows)
        for k in range(count):
            half_ref[k, span] = piece[k]
    span = pl.ds(first_row(at_ref, REACH, rows), rows)
    for k in range(count):
        half_ref[k, span] = jnp.zeros((rows, vec), BF16)
        both = jnp.dot(terms_ref[k], half_ref[k], preferred_element_type=F32)
        total_ref[k * vec : (k + 1) * vec] = both[:vec] + both[vec:]


def early(at, terms, pieces):
    count, rows, vec = pieces[0].shape
    shapes = [jax.ShapeDtypeStruct((count * vec, vec), F32), jax.ShapeDtypeStruct((count, RING * rows, vec), BF16)]
    specs = [SMEM] + [VMEM] * (1 + len(pieces))
    return call(early_kernel, (at, terms, *pieces), specs, [VMEM, VMEM], shapes, 4 * count * RING * rows * vec * vec)


def late_kernel(at_ref, terms_ref, total_ref, half_ref, piece_ref, out_ref, whole_ref):
    count, rows, vec = piece_ref.shape
    span = pl.ds(first_row(at_ref, REACH, rows), rows)
    for k in range(count):
        both = jnp.dot(terms_ref[k, :, span], piece_ref[k], preferred_element_type=F32)
        panel = slice(k * vec, (k + 1) * vec)
        out_ref[panel] = total_ref[panel] + both[:vec] + both[vec:]
        whole_ref[k] = half_ref[k]
        whole_ref[k, span] = piece_ref[k]


def late(at, terms, total, half, piece):
    shapes = [jax.ShapeDtypeStruct(total.shape, F32), jax.ShapeDtypeStruct(half.shape, BF16)]
    return call(late_kernel, (at, terms, total, half, piece), [SMEM] + [VMEM] * 4, [VMEM, VMEM], shapes)


def spread_kernel(part_ref, out_ref, token_ref):
    total = jnp.sum(part_ref[...], axis=0)
    for j in range(RING):
        out_ref[j] = total
    token_ref[...] = jnp.zeros_like(token_ref)


def spread(parts):
    return call(spread_kernel, (parts,), [VMEM], [VMEM] * 2, [jax.ShapeDtypeStruct((RING,) + parts.shape[1:], F32), TOKEN])


def scale_kernel(parts_ref, below_ref, _, out_ref):
    out_ref[...] = (jnp.sum(parts_ref[...], axis=0) / below_ref[...]).astype(BF16)


def apply_kernel(at_ref, own_ref, other_ref, scaled_ref, panels_ref, out_ref, fetched_ref, block_ref, in_sems, out_sems):
    steps, size, _ = block_ref.shape
    count, half, _ = own_ref.shape
    near = steps // 2
    fetches, copies = [], []
    for number in range(steps):
        ref = own_ref if number < near else other_ref
        rows = pl.ds((number % near) * size, size)
        fetches.append(pltpu.make_async_copy(ref.at[:, rows], fetched_ref.at[number], in_sems.at[number]))
        fetches[-1].start()
    for number in range(steps):
        fetches[number].wait()
        total = None
        for k in range(count):
            rotated = lax.dot_general(fetched_ref[number, k], scaled_ref[k], (((1,), (1,)), ((), ())), preferred_element_type=F32)
            term = lax.dot_general(rotated.astype(BF16), panels_ref[k], (((1,), (1,)), ((), ())), preferred_element_type=F32)
            total = term if total is None else total + term
        block_ref[number] = total.astype(BF16)
        first = at_ref[0] if number < near else 1 - at_ref[0]
        rows = half // RING
        for i in range(size // rows):
            target = pl.multiple_of((((number % near) * size // rows + i) * 2 + first) * rows, rows)
            source = block_ref.at[number, pl.ds(i * rows, rows)]
            copies.append(pltpu.make_async_copy(source, out_ref.at[pl.ds(target, rows)], out_sems.at[len(copies)]))
            copies[-1].start()
    for copy in copies:
        copy.wait()


def apply(at, own, other, scaled, panels):
    count, rows, vec = other.shape
    width = panels.shape[1]
    steps = 4
    size = 2 * rows // steps
    return call(
        apply_kernel,
        (at, own, other, scaled, panels),
        [SMEM, ANY, ANY, VMEM, VMEM],
        ANY,
        jax.ShapeDtypeStruct((2 * rows, width), BF16),
        4 * count * rows * vec * (vec + width),
        [
            pltpu.VMEM((steps, count, size, vec), BF16),
            pltpu.VMEM((steps, size, width), BF16),
            pltpu.SemaphoreType.DMA((steps,)),
            pltpu.SemaphoreType.DMA((2 * RING,)),
        ],
        limit=24,
    )


def body(gradient, in_panels, out_pool, eigenvalues, owners):
    core, high, here = (lax.axis_index(a) for a in ("core", "yh", "z"))
    at = jnp.concatenate([jnp.stack([core, high, here, lax.axis_index(PLANE)]).astype(jnp.int32), owners])
    count, _, vec = in_panels.shape
    size = out_pool.shape[1] // RING
    piece = jax.ShapeDtypeStruct((count, size // 2, vec), BF16)

    with jax.named_scope("scatter"):
        every = lax.all_to_all(out_pool.reshape(RING, size, vec), "z", 0, 0)

    with jax.named_scope("projection"):
        sent, one = project(at, False, gradient, in_panels)
        kept, two = project(at, True, gradient, in_panels)

    with jax.named_scope("gather"):
        scratch = [pltpu.SemaphoreType.DMA((2 * count,))]
        specs = [SMEM, ANY, ANY, ANY]
        mine, send = call(pick_kernel, (at, every, one, two), specs, [VMEM] * 2, [piece] * 2, scratch=scratch)
        mine, token = level(0, at, mine, swap(send, "core"))
        sent, token = lax.optimization_barrier((sent, token))
        terms, below = split(at, kept, swap(sent, "core"), eigenvalues, 32, token)
        mine, _ = level(1, at, mine, swap(mine, "yh"))
        pieces = [mine]
        up = down = mine
        for _ in range(1, REACH):
            up, down = shift(up, 1), shift(down, -1)
            pieces += [up, down]
        pieces.append(shift(up, 1))

    with jax.named_scope("coupling"):
        part, own = early(at, terms, pieces[:-1])
        part, own = late(at, terms, part, own, pieces[-1])
        part, token = spread(lax.all_to_all(part.reshape(32, -1, vec), PLANE, 0, 0))
        own, token = lax.optimization_barrier((own, token))
        other = swap(own, "core")
        part = lax.all_to_all(part, "z", 0, 0)
        scaled = call(scale_kernel, (part, below, token), [VMEM, VMEM, ANY], VMEM, jax.ShapeDtypeStruct(part.shape[1:], BF16))
        copies = jnp.broadcast_to(scaled[None], (32,) + scaled.shape)
        scaled = lax.all_to_all(copies, PLANE, 0, 0).reshape(count, vec, vec)

    with jax.named_scope("output"):
        return apply(at, own, other, scaled, in_panels)


def solution(mesh):
    fine = Mesh(mesh.devices.reshape(2, 4, 2, 8, 2), ROW + COL)
    return jax.shard_map(
        body,
        mesh=fine,
        in_specs=(P(ROW, COL), P(None, COL, None), P(COL, ROW, None), P(), P()),
        out_specs=P(ROW, COL),
        check_vma=False,
    )
```

```python
import functools

import jax
import jax.numpy as jnp
from jax import lax
from jax.experimental import pallas as pl
from jax.experimental.pallas import tpu as pltpu
from jax.sharding import Mesh
from jax.sharding import PartitionSpec as P

ROW = ("yl", "x")
COL = ("yh", "z", "core")
PLANE = ("core", "yl", "x", "yh")
F32 = jnp.float32
BF16 = jnp.bfloat16
RING = 8
REACH = RING // 2
MIB = 1024 * 1024

VMEM = pl.BlockSpec(memory_space=pltpu.VMEM)
SMEM = pl.BlockSpec(memory_space=pltpu.SMEM)
ANY = pl.BlockSpec(memory_space=pl.ANY)
TOKEN = jax.ShapeDtypeStruct((8, 128), F32)


def swap(x, axis):
    return lax.ppermute(x, axis, [(0, 1), (1, 0)])


def shift(x, by):
    return lax.ppermute(x, "z", [(i, (i + by) % RING) for i in range(RING)])


def call(kernel, args, in_specs, out_specs, out_shape, flops=0, scratch=(), limit=16):
    moved = sum(a.size * a.dtype.itemsize for a in args)
    return pl.pallas_call(
        kernel,
        in_specs=in_specs,
        out_specs=out_specs,
        out_shape=out_shape,
        scratch_shapes=scratch,
        compiler_params=pltpu.CompilerParams(vmem_limit_bytes=limit * MIB),
        cost_estimate=pl.CostEstimate(flops=flops, bytes_accessed=moved, transcendentals=0),
    )(*args)


def owner_of(at_ref, k):
    number = at_ref[4 + k]
    return number & 1, (number >> 1) & (RING - 1), number >> 4


def pick_kernel(at_ref, all_ref, _one, _two, keep_ref, send_ref, sems):
    rows = keep_ref.shape[1]
    copies = []
    for k in range(keep_ref.shape[0]):
        _, place, high = owner_of(at_ref, k)
        for half, ref in ((at_ref[0], keep_ref), (1 - at_ref[0], send_ref)):
            span = pl.ds(pl.multiple_of(half * rows, rows), rows)
            copies.append(pltpu.make_async_copy(all_ref.at[place * 2 + high, span], ref.at[k], sems.at[len(copies)]))
            copies[-1].start()
    for copy in copies:
        copy.wait()


def level_kernel(at_ref, mine_ref, other_ref, out_ref):
    for k in range(out_ref.shape[0]):
        core, _, _ = owner_of(at_ref, k)

        @pl.when(core == at_ref[0])
        def _():
            out_ref[k] = mine_ref[k]

        @pl.when(core != at_ref[0])
        def _():
            out_ref[k] = other_ref[k]


def level(at, mine, other):
    return call(level_kernel, (at, mine, other), [SMEM, VMEM, VMEM], VMEM, jax.ShapeDtypeStruct(mine.shape, mine.dtype))


def project_kernel(own, at_ref, gradient_ref, panels_ref, *refs):
    outs, (token_ref, rows_ref, sems) = refs[:-3], refs[-3:]
    size = rows_ref.shape[0] // (2 * RING)
    half = at_ref[0] if own else 1 - at_ref[0]
    copies = []
    for high in range(2):
        for place in range(RING):
            start = pl.multiple_of((place * 4 + high * 2 + half) * size, size)
            target = rows_ref.at[pl.ds(len(copies) * size, size)]
            copies.append(pltpu.make_async_copy(gradient_ref.at[pl.ds(start, size)], target, sems.at[len(copies)]))
            copies[-1].start()
    for i in range(0, len(copies), 4):
        for copy in copies[i : i + 4]:
            copy.wait()
        span = slice(i * size, (i + 4) * size)
        for k, out_ref in enumerate(outs):
            out_ref[span] = jnp.dot(rows_ref[span], panels_ref[k], preferred_element_type=F32)
    token_ref[...] = jnp.zeros_like(token_ref)


def project(at, own, gradient, panels):
    count, width, vec = panels.shape
    rows = gradient.shape[0] // 2
    *outs, token = call(
        functools.partial(project_kernel, own),
        (at, gradient, panels),
        [SMEM, ANY, VMEM],
        [VMEM] * (count + 1),
        [jax.ShapeDtypeStruct((rows, vec), F32)] * count + [TOKEN],
        2 * rows * width * vec * count,
        [pltpu.VMEM((rows, width), BF16), pltpu.SemaphoreType.DMA((2 * RING,))],
    )
    return outs, token


def pool_kernel(count, at_ref, *refs):
    kept, came, keeps = (refs[i * count : (i + 1) * count] for i in range(3))
    send_ref, token_ref = refs[3 * count :]
    rows = keeps[0].shape[0]
    mine = pl.ds(pl.multiple_of(at_ref[1] * rows, rows), rows)
    other = pl.ds(pl.multiple_of((1 - at_ref[1]) * rows, rows), rows)
    for k in range(count):
        keeps[k][...] = kept[k][mine] + came[k][mine]
        send_ref[k] = (kept[k][other] + came[k][other]).astype(BF16)
    token_ref[...] = jnp.zeros_like(token_ref)


def pool(at, kept, came):
    count = len(kept)
    rows, vec = kept[0].shape
    shapes = [jax.ShapeDtypeStruct((rows // 2, vec), F32)] * count + [jax.ShapeDtypeStruct((count, rows // 2, vec), BF16), TOKEN]
    out = call(functools.partial(pool_kernel, count), (at, *kept, *came), [SMEM] + [VMEM] * (2 * count), [VMEM] * (count + 2), shapes)
    return out[:count], out[count], out[count + 1]


def split_kernel(count, at_ref, values_ref, *refs):
    kept, (came_ref, out_ref, below_ref, all_ref) = refs[:count], refs[count:]
    vec = kept[0].shape[1]
    for k in range(count):
        total = (kept[k][...] + came_ref[k].astype(F32)).T
        high = total.astype(BF16)
        out_ref[k, :vec] = high
        out_ref[k, vec:] = (total - high.astype(F32)).astype(BF16)
        values = values_ref[k]
        all_ref[k * vec : (k + 1) * vec] = (values + 0.1 * jnp.mean(values)).T
    size = below_ref.shape[0]
    below_ref[...] = all_ref[pl.ds(pl.multiple_of(at_ref[3] * size, size), size)]


def split(at, values, kept, came, places):
    count = len(kept)
    rows, vec = kept[0].shape
    shapes = [jax.ShapeDtypeStruct((count, 2 * vec, rows), BF16), jax.ShapeDtypeStruct((count * vec // places, vec), F32)]
    specs = [SMEM] + [VMEM] * (2 + count)
    return call(functools.partial(split_kernel, count), (at, values, *kept, came), specs, [VMEM] * 2, shapes, scratch=[pltpu.VMEM((count * vec, vec), F32)])


def offsets():
    order = [0]
    for step in range(1, REACH + 1):
        order.append(-step)
        if step < REACH:
            order.append(step)
    return order


def couple_kernel(at_ref, terms_ref, *refs):
    pieces, (total_ref, own_ref) = refs[:RING], refs[RING:]
    count, rows, vec = pieces[0].shape
    for piece, offset in zip(pieces, offsets()):
        place = (at_ref[2] + offset + RING) & (RING - 1)
        span = pl.ds(pl.multiple_of(place * rows, rows), rows)
        for k in range(count):
            own_ref[k, span] = piece[k]
    for k in range(count):
        both = jnp.dot(terms_ref[k], own_ref[k], preferred_element_type=F32)
        total_ref[k * vec : (k + 1) * vec] = both[:vec] + both[vec:]


def couple(at, terms, pieces):
    count, rows, vec = pieces[0].shape
    shapes = [jax.ShapeDtypeStruct((count * vec, vec), F32), jax.ShapeDtypeStruct((count, RING * rows, vec), BF16)]
    return call(couple_kernel, (at, terms, *pieces), [SMEM] + [VMEM] * (1 + RING), [VMEM, VMEM], shapes, 4 * count * RING * rows * vec * vec)


def spread_kernel(part_ref, out_ref, token_ref):
    total = jnp.sum(part_ref[...], axis=0)
    for j in range(RING):
        out_ref[j] = total
    token_ref[...] = jnp.zeros_like(token_ref)


def spread(parts):
    return call(spread_kernel, (parts,), [VMEM], [VMEM] * 2, [jax.ShapeDtypeStruct((RING,) + parts.shape[1:], F32), TOKEN])


def scale_kernel(parts_ref, below_ref, _, out_ref):
    out_ref[...] = (jnp.sum(parts_ref[...], axis=0) / below_ref[...]).astype(BF16)


def apply_kernel(near, at_ref, own_ref, other_ref, scaled_ref, panels_ref, _, out_ref, block_ref, sems):
    count, rows, _ = own_ref.shape
    size = rows // RING
    high = at_ref[1] if near else 1 - at_ref[1]
    copies = []
    for number, (ref, core) in enumerate(((own_ref, at_ref[0]), (other_ref, 1 - at_ref[0]))):
        total = None
        for k in range(count):
            rotated = lax.dot_general(ref[k], scaled_ref[k], (((1,), (1,)), ((), ())), preferred_element_type=F32)
            term = lax.dot_general(rotated.astype(BF16), panels_ref[k], (((1,), (1,)), ((), ())), preferred_element_type=F32)
            total = term if total is None else total + term
        block_ref[number] = total.astype(BF16)
        for place in range(RING):
            target = pl.multiple_of((place * 4 + high * 2 + core) * size, size)
            source = block_ref.at[number, pl.ds(place * size, size)]
            copies.append(pltpu.make_async_copy(source, out_ref.at[pl.ds(target, size)], sems.at[len(copies)]))
            copies[-1].start()
    for copy in copies:
        copy.wait()


def apply(near, at, own, other, scaled, panels, into):
    count, rows, vec = own.shape
    width = panels.shape[1]
    return pl.pallas_call(
        functools.partial(apply_kernel, near),
        in_specs=[SMEM, VMEM, VMEM, VMEM, VMEM, ANY],
        out_specs=ANY,
        out_shape=jax.ShapeDtypeStruct((4 * rows, width), BF16),
        input_output_aliases={} if near else {5: 0},
        scratch_shapes=[pltpu.VMEM((2, rows, width), BF16), pltpu.SemaphoreType.DMA((2 * RING,))],
        compiler_params=pltpu.CompilerParams(vmem_limit_bytes=24 * MIB),
        cost_estimate=pl.CostEstimate(flops=4 * count * rows * vec * (vec + width), bytes_accessed=4 * rows * width, transcendentals=0),
    )(at, own, other, scaled, panels, into)


def body(gradient, in_panels, out_pool, eigenvalues, owners):
    core, high, here = (lax.axis_index(a) for a in ("core", "yh", "z"))
    at = jnp.concatenate([jnp.stack([core, high, here, lax.axis_index(PLANE)]).astype(jnp.int32), owners])
    count, _, vec = in_panels.shape
    size = out_pool.shape[1] // (4 * RING)
    piece = jax.ShapeDtypeStruct((count, size, vec), BF16)

    with jax.named_scope("scatter"):
        every = lax.all_to_all(out_pool.reshape(2 * RING, 2 * size, vec), ("z", "yh"), 0, 0)

    with jax.named_scope("projection"):
        sent, _ = project(at, False, gradient, in_panels)
        kept, one = project(at, True, gradient, in_panels)
        kept, sent, two = pool(at, kept, [swap(x, "core") for x in sent])
        terms, below = split(at, eigenvalues, kept, swap(sent, "yh"), 32)

    with jax.named_scope("gather"):
        scratch = [pltpu.SemaphoreType.DMA((2 * count,))]
        specs = [SMEM, ANY, ANY, ANY]
        mine, send = call(pick_kernel, (at, every, one, two), specs, [VMEM] * 2, [piece] * 2, scratch=scratch)
        mine = level(at, mine, swap(send, "core"))
        pieces = [mine]
        up = down = mine
        for _ in range(1, REACH):
            up, down = shift(up, 1), shift(down, -1)
            pieces += [up, down]
        pieces.append(shift(up, 1))

    with jax.named_scope("coupling"):
        part, own = couple(at, terms, pieces)
        part, token = spread(lax.all_to_all(part.reshape(32, -1, vec), PLANE, 0, 0))
        own, token = lax.optimization_barrier((own, token))
        far, other = swap(own, "yh"), swap(own, "core")
        part = lax.all_to_all(part, "z", 0, 0)
        scaled = call(scale_kernel, (part, below, token), [VMEM, VMEM, ANY], VMEM, jax.ShapeDtypeStruct(part.shape[1:], BF16))
        copies = jnp.broadcast_to(scaled[None], (32,) + scaled.shape)
        scaled = lax.all_to_all(copies, PLANE, 0, 0).reshape(count, vec, vec)

    with jax.named_scope("output"):
        far, token = lax.optimization_barrier((far, scaled[0, :16, :128]))
        out = apply(True, at, own, other, scaled, in_panels, token)
        return apply(False, at, far, swap(far, "core"), scaled, in_panels, out)


def solution(mesh):
    fine = Mesh(mesh.devices.reshape(2, 4, 2, 8, 2), ROW + COL)
    return jax.shard_map(
        body,
        mesh=fine,
        in_specs=(P(ROW, COL), P(None, COL, None), P(COL, ROW, None), P(), P()),
        out_specs=P(ROW, COL),
        check_vma=False,
    )
```

```python
import functools

import jax
import jax.numpy as jnp
from jax import lax
from jax.experimental import pallas as pl
from jax.experimental.pallas import tpu as pltpu
from jax.sharding import Mesh
from jax.sharding import PartitionSpec as P

ROW = ("yl", "x")
COL = ("yh", "z", "core")
PLANE = ("core", "yl", "x", "yh")
F32 = jnp.float32
BF16 = jnp.bfloat16
RING = 8
REACH = RING // 2
MIB = 1024 * 1024

VMEM = pl.BlockSpec(memory_space=pltpu.VMEM)
SMEM = pl.BlockSpec(memory_space=pltpu.SMEM)
ANY = pl.BlockSpec(memory_space=pl.ANY)
TOKEN = jax.ShapeDtypeStruct((8, 128), F32)


def swap(x, axis):
    return lax.ppermute(x, axis, [(0, 1), (1, 0)])


def shift(x, by):
    return lax.ppermute(x, "z", [(i, (i + by) % RING) for i in range(RING)])


def call(kernel, args, in_specs, out_specs, out_shape, flops=0, scratch=(), limit=16):
    moved = sum(a.size * a.dtype.itemsize for a in args)
    return pl.pallas_call(
        kernel,
        in_specs=in_specs,
        out_specs=out_specs,
        out_shape=out_shape,
        scratch_shapes=scratch,
        compiler_params=pltpu.CompilerParams(vmem_limit_bytes=limit * MIB),
        cost_estimate=pl.CostEstimate(flops=flops, bytes_accessed=moved, transcendentals=0),
    )(*args)


def owner_of(at_ref, k):
    number = at_ref[4 + k]
    return number & 1, (number >> 1) & (RING - 1), number >> 4


def pick_kernel(at_ref, all_ref, _one, _two, keep_ref, send_ref, sems):
    rows = keep_ref.shape[1]
    copies = []
    for k in range(keep_ref.shape[0]):
        _, place, high = owner_of(at_ref, k)
        for half, ref in ((at_ref[0], keep_ref), (1 - at_ref[0], send_ref)):
            span = pl.ds(pl.multiple_of(half * rows, rows), rows)
            copies.append(pltpu.make_async_copy(all_ref.at[place * 2 + high, span], ref.at[k], sems.at[len(copies)]))
            copies[-1].start()
    for copy in copies:
        copy.wait()


def level_kernel(at_ref, mine_ref, other_ref, out_ref):
    for k in range(out_ref.shape[0]):
        core, _, _ = owner_of(at_ref, k)

        @pl.when(core == at_ref[0])
        def _():
            out_ref[k] = mine_ref[k]

        @pl.when(core != at_ref[0])
        def _():
            out_ref[k] = other_ref[k]


def level(at, mine, other):
    return call(level_kernel, (at, mine, other), [SMEM, VMEM, VMEM], VMEM, jax.ShapeDtypeStruct(mine.shape, mine.dtype))


def project_kernel(own, at_ref, gradient_ref, panels_ref, *refs):
    outs, (token_ref, rows_ref, sems) = refs[:-3], refs[-3:]
    size = rows_ref.shape[0] // (2 * RING)
    half = at_ref[0] if own else 1 - at_ref[0]
    copies = []
    for high in range(2):
        for place in range(RING):
            start = pl.multiple_of((place * 4 + high * 2 + half) * size, size)
            target = rows_ref.at[pl.ds(len(copies) * size, size)]
            copies.append(pltpu.make_async_copy(gradient_ref.at[pl.ds(start, size)], target, sems.at[len(copies)]))
            copies[-1].start()
    for i in range(0, len(copies), 4):
        for copy in copies[i : i + 4]:
            copy.wait()
        span = slice(i * size, (i + 4) * size)
        for k, out_ref in enumerate(outs):
            out_ref[span] = jnp.dot(rows_ref[span], panels_ref[k], preferred_element_type=F32)
    token_ref[...] = jnp.zeros_like(token_ref)


def project(at, own, gradient, panels):
    count, width, vec = panels.shape
    rows = gradient.shape[0] // 2
    *outs, token = call(
        functools.partial(project_kernel, own),
        (at, gradient, panels),
        [SMEM, ANY, VMEM],
        [VMEM] * (count + 1),
        [jax.ShapeDtypeStruct((rows, vec), F32)] * count + [TOKEN],
        2 * rows * width * vec * count,
        [pltpu.VMEM((rows, width), BF16), pltpu.SemaphoreType.DMA((2 * RING,))],
    )
    return outs, token


def pool_kernel(count, at_ref, *refs):
    kept, came = refs[:count], refs[count : 2 * count]
    keep_ref, send_ref, token_ref = refs[2 * count :]
    rows = keep_ref.shape[1]
    mine = pl.ds(pl.multiple_of(at_ref[1] * rows, rows), rows)
    other = pl.ds(pl.multiple_of((1 - at_ref[1]) * rows, rows), rows)
    for k in range(count):
        keep_ref[k] = kept[k][mine] + came[k][mine]
        send_ref[k] = (kept[k][other] + came[k][other]).astype(BF16)
    token_ref[...] = jnp.zeros_like(token_ref)


def pool(at, kept, came):
    count = len(kept)
    rows, vec = kept[0].shape
    half = (count, rows // 2, vec)
    shapes = [jax.ShapeDtypeStruct(half, F32), jax.ShapeDtypeStruct(half, BF16), TOKEN]
    return call(functools.partial(pool_kernel, count), (at, *kept, *came), [SMEM] + [VMEM] * (2 * count), [VMEM] * 3, shapes)


def split_kernel(at_ref, values_ref, kept_ref, came_ref, out_ref, below_ref, all_ref):
    count, _, vec = kept_ref.shape
    for k in range(count):
        total = (kept_ref[k] + came_ref[k].astype(F32)).T
        high = total.astype(BF16)
        out_ref[k, :vec] = high
        out_ref[k, vec:] = (total - high.astype(F32)).astype(BF16)
        values = values_ref[k]
        all_ref[k * vec : (k + 1) * vec] = (values + 0.1 * jnp.mean(values)).T
    size = below_ref.shape[0]
    below_ref[...] = all_ref[pl.ds(pl.multiple_of(at_ref[3] * size, size), size)]


def split(at, values, kept, came, places):
    count, rows, vec = kept.shape
    shapes = [jax.ShapeDtypeStruct((count, 2 * vec, rows), BF16), jax.ShapeDtypeStruct((count * vec // places, vec), F32)]
    return call(split_kernel, (at, values, kept, came), [SMEM] + [VMEM] * 3, [VMEM] * 2, shapes, scratch=[pltpu.VMEM((count * vec, vec), F32)])


def offsets():
    order = [0]
    for step in range(1, REACH + 1):
        order.append(-step)
        if step < REACH:
            order.append(step)
    return order


def couple_kernel(at_ref, terms_ref, *refs):
    pieces, (total_ref, own_ref) = refs[:RING], refs[RING:]
    count, rows, vec = pieces[0].shape
    for piece, offset in zip(pieces, offsets()):
        place = (at_ref[2] + offset + RING) & (RING - 1)
        span = pl.ds(pl.multiple_of(place * rows, rows), rows)
        for k in range(count):
            own_ref[k, span] = piece[k]
    for k in range(count):
        both = jnp.dot(terms_ref[k], own_ref[k], preferred_element_type=F32)
        total_ref[k * vec : (k + 1) * vec] = both[:vec] + both[vec:]


def couple(at, terms, pieces):
    count, rows, vec = pieces[0].shape
    shapes = [jax.ShapeDtypeStruct((count * vec, vec), F32), jax.ShapeDtypeStruct((count, RING * rows, vec), BF16)]
    return call(couple_kernel, (at, terms, *pieces), [SMEM] + [VMEM] * (1 + RING), [VMEM, VMEM], shapes, 4 * count * RING * rows * vec * vec)


def spread_kernel(part_ref, below_ref, out_ref, token_ref):
    total = jnp.sum(part_ref[...], axis=0) / below_ref[...]
    for j in range(RING):
        out_ref[j] = total
    token_ref[...] = jnp.zeros_like(token_ref)


def spread(parts, below):
    return call(spread_kernel, (parts, below), [VMEM, VMEM], [VMEM] * 2, [jax.ShapeDtypeStruct((RING,) + parts.shape[1:], F32), TOKEN])


def scale_kernel(parts_ref, _, out_ref):
    out_ref[...] = jnp.sum(parts_ref[...], axis=0).astype(BF16)


def apply_kernel(near, at_ref, own_ref, other_ref, scaled_ref, panels_ref, _, out_ref, block_ref, sems):
    count, rows, _ = own_ref.shape
    size = rows // RING
    high = at_ref[1] if near else 1 - at_ref[1]
    copies = []
    for number, (ref, core) in enumerate(((own_ref, at_ref[0]), (other_ref, 1 - at_ref[0]))):
        total = None
        for k in range(count):
            rotated = lax.dot_general(ref[k], scaled_ref[k], (((1,), (1,)), ((), ())), preferred_element_type=F32)
            term = lax.dot_general(rotated.astype(BF16), panels_ref[k], (((1,), (1,)), ((), ())), preferred_element_type=F32)
            total = term if total is None else total + term
        block_ref[number] = total.astype(BF16)
        for place in range(RING):
            target = pl.multiple_of((place * 4 + high * 2 + core) * size, size)
            source = block_ref.at[number, pl.ds(place * size, size)]
            copies.append(pltpu.make_async_copy(source, out_ref.at[pl.ds(target, size)], sems.at[len(copies)]))
            copies[-1].start()
    for copy in copies:
        copy.wait()


def apply(near, at, own, other, scaled, panels, into):
    count, rows, vec = own.shape
    width = panels.shape[1]
    return pl.pallas_call(
        functools.partial(apply_kernel, near),
        in_specs=[SMEM, VMEM, VMEM, VMEM, VMEM, ANY],
        out_specs=ANY,
        out_shape=jax.ShapeDtypeStruct((4 * rows, width), BF16),
        input_output_aliases={} if near else {5: 0},
        scratch_shapes=[pltpu.VMEM((2, rows, width), BF16), pltpu.SemaphoreType.DMA((2 * RING,))],
        compiler_params=pltpu.CompilerParams(vmem_limit_bytes=24 * MIB),
        cost_estimate=pl.CostEstimate(flops=4 * count * rows * vec * (vec + width), bytes_accessed=4 * rows * width, transcendentals=0),
    )(at, own, other, scaled, panels, into)


def body(gradient, in_panels, out_pool, eigenvalues, owners):
    core, high, here = (lax.axis_index(a) for a in ("core", "yh", "z"))
    at = jnp.concatenate([jnp.stack([core, high, here, lax.axis_index(PLANE)]).astype(jnp.int32), owners])
    count, _, vec = in_panels.shape
    size = out_pool.shape[1] // (4 * RING)
    piece = jax.ShapeDtypeStruct((count, size, vec), BF16)

    with jax.named_scope("scatter"):
        every = lax.all_to_all(out_pool.reshape(2 * RING, 2 * size, vec), ("z", "yh"), 0, 0)

    with jax.named_scope("projection"):
        sent, _ = project(at, False, gradient, in_panels)
        kept, one = project(at, True, gradient, in_panels)
        kept, sent, two = pool(at, kept, [swap(x, "core") for x in sent])
        terms, below = split(at, eigenvalues, kept, swap(sent, "yh"), 32)

    with jax.named_scope("gather"):
        scratch = [pltpu.SemaphoreType.DMA((2 * count,))]
        specs = [SMEM, ANY, ANY, ANY]
        mine, send = call(pick_kernel, (at, every, one, two), specs, [VMEM] * 2, [piece] * 2, scratch=scratch)
        mine = level(at, mine, swap(send, "core"))
        pieces = [mine]
        up = down = mine
        for _ in range(1, REACH):
            up, down = shift(up, 1), shift(down, -1)
            pieces += [up, down]
        pieces.append(shift(up, 1))

    with jax.named_scope("coupling"):
        part, own = couple(at, terms, pieces)
        part, token = spread(lax.all_to_all(part.reshape(32, -1, vec), PLANE, 0, 0), below)
        own, token = lax.optimization_barrier((own, token))
        far, other = swap(own, "yh"), swap(own, "core")
        part = lax.all_to_all(part, "z", 0, 0)
        scaled = call(scale_kernel, (part, token), [VMEM, ANY], VMEM, jax.ShapeDtypeStruct(part.shape[1:], BF16))
        copies = jnp.broadcast_to(scaled[None], (32,) + scaled.shape)
        scaled = lax.all_to_all(copies, PLANE, 0, 0).reshape(count, vec, vec)

    with jax.named_scope("output"):
        far, token = lax.optimization_barrier((far, scaled[0, :16, :128]))
        out = apply(True, at, own, other, scaled, in_panels, token)
        return apply(False, at, far, swap(far, "core"), scaled, in_panels, out)


def solution(mesh):
    fine = Mesh(mesh.devices.reshape(2, 4, 2, 8, 2), ROW + COL)
    return jax.shard_map(
        body,
        mesh=fine,
        in_specs=(P(ROW, COL), P(None, COL, None), P(COL, ROW, None), P(), P()),
        out_specs=P(ROW, COL),
        check_vma=False,
    )
```

```python
import functools

import jax
import jax.numpy as jnp
from jax import lax
from jax.experimental import pallas as pl
from jax.experimental.pallas import tpu as pltpu
from jax.sharding import Mesh
from jax.sharding import PartitionSpec as P

ROW = ("yl", "x")
COL = ("yh", "z", "core")
PLANE = ("core", "yl", "x", "yh")
F32 = jnp.float32
BF16 = jnp.bfloat16
RING = 8
REACH = RING // 2
MIB = 1024 * 1024

VMEM = pl.BlockSpec(memory_space=pltpu.VMEM)
SMEM = pl.BlockSpec(memory_space=pltpu.SMEM)
ANY = pl.BlockSpec(memory_space=pl.ANY)
TOKEN = jax.ShapeDtypeStruct((8, 128), F32)


def swap(x, axis):
    return lax.ppermute(x, axis, [(0, 1), (1, 0)])


def shift(x, by):
    return lax.ppermute(x, "z", [(i, (i + by) % RING) for i in range(RING)])


def call(kernel, args, in_specs, out_specs, out_shape, flops=0, scratch=(), limit=16):
    moved = sum(a.size * a.dtype.itemsize for a in args)
    return pl.pallas_call(
        kernel,
        in_specs=in_specs,
        out_specs=out_specs,
        out_shape=out_shape,
        scratch_shapes=scratch,
        compiler_params=pltpu.CompilerParams(vmem_limit_bytes=limit * MIB),
        cost_estimate=pl.CostEstimate(flops=flops, bytes_accessed=moved, transcendentals=0),
    )(*args)


def owner_of(at_ref, k):
    number = at_ref[4 + k]
    return number & 1, (number >> 1) & (RING - 1), number >> 4


def pick_kernel(at_ref, all_ref, _one, _two, keep_ref, send_ref, sems):
    rows = keep_ref.shape[1]
    copies = []
    for k in range(keep_ref.shape[0]):
        _, place, high = owner_of(at_ref, k)
        for half, ref in ((at_ref[0], keep_ref), (1 - at_ref[0], send_ref)):
            span = pl.ds(pl.multiple_of(half * rows, rows), rows)
            copies.append(pltpu.make_async_copy(all_ref.at[place * 2 + high, span], ref.at[k], sems.at[len(copies)]))
            copies[-1].start()
    for copy in copies:
        copy.wait()


def level_kernel(at_ref, mine_ref, other_ref, out_ref):
    for k in range(out_ref.shape[0]):
        core, _, _ = owner_of(at_ref, k)

        @pl.when(core == at_ref[0])
        def _():
            out_ref[k] = mine_ref[k]

        @pl.when(core != at_ref[0])
        def _():
            out_ref[k] = other_ref[k]


def level(at, mine, other):
    return call(level_kernel, (at, mine, other), [SMEM, VMEM, VMEM], VMEM, jax.ShapeDtypeStruct(mine.shape, mine.dtype))


def project_kernel(own, at_ref, gradient_ref, panels_ref, *refs):
    outs, (token_ref, rows_ref, sems) = refs[:-3], refs[-3:]
    size = rows_ref.shape[0] // (2 * RING)
    half = at_ref[0] if own else 1 - at_ref[0]
    copies = []
    for high in range(2):
        for place in range(RING):
            start = pl.multiple_of((place * 4 + high * 2 + half) * size, size)
            target = rows_ref.at[pl.ds(len(copies) * size, size)]
            copies.append(pltpu.make_async_copy(gradient_ref.at[pl.ds(start, size)], target, sems.at[len(copies)]))
            copies[-1].start()
    for i in range(0, len(copies), 4):
        for copy in copies[i : i + 4]:
            copy.wait()
        span = slice(i * size, (i + 4) * size)
        for k, out_ref in enumerate(outs):
            out_ref[span] = jnp.dot(rows_ref[span], panels_ref[k], preferred_element_type=F32)
    token_ref[...] = jnp.zeros_like(token_ref)


def project(at, own, gradient, panels):
    count, width, vec = panels.shape
    rows = gradient.shape[0] // 2
    *outs, token = call(
        functools.partial(project_kernel, own),
        (at, gradient, panels),
        [SMEM, ANY, VMEM],
        [VMEM] * (count + 1),
        [jax.ShapeDtypeStruct((rows, vec), F32)] * count + [TOKEN],
        2 * rows * width * vec * count,
        [pltpu.VMEM((rows, width), BF16), pltpu.SemaphoreType.DMA((2 * RING,))],
    )
    return outs, token


def pool_kernel(count, at_ref, *refs):
    kept, came = refs[:count], refs[count : 2 * count]
    keep_ref, send_ref, token_ref = refs[2 * count :]
    rows = keep_ref.shape[1]
    mine = pl.ds(pl.multiple_of(at_ref[1] * rows, rows), rows)
    other = pl.ds(pl.multiple_of((1 - at_ref[1]) * rows, rows), rows)
    for k in range(count):
        keep_ref[k] = kept[k][mine] + came[k][mine]
        send_ref[k] = (kept[k][other] + came[k][other]).astype(BF16)
    token_ref[...] = jnp.zeros_like(token_ref)


def pool(at, kept, came):
    count = len(kept)
    rows, vec = kept[0].shape
    half = (count, rows // 2, vec)
    shapes = [jax.ShapeDtypeStruct(half, F32), jax.ShapeDtypeStruct(half, BF16), TOKEN]
    return call(functools.partial(pool_kernel, count), (at, *kept, *came), [SMEM] + [VMEM] * (2 * count), [VMEM] * 3, shapes)


def split_kernel(at_ref, values_ref, kept_ref, came_ref, out_ref, below_ref, all_ref):
    count, _, vec = kept_ref.shape
    for k in range(count):
        total = (kept_ref[k] + came_ref[k].astype(F32)).T
        high = total.astype(BF16)
        out_ref[k, :vec] = high
        out_ref[k, vec:] = (total - high.astype(F32)).astype(BF16)
        values = values_ref[k]
        all_ref[k * vec : (k + 1) * vec] = (values + 0.1 * jnp.mean(values)).T
    size = below_ref.shape[0]
    below_ref[...] = all_ref[pl.ds(pl.multiple_of(at_ref[3] * size, size), size)]


def split(at, values, kept, came, places):
    count, rows, vec = kept.shape
    shapes = [jax.ShapeDtypeStruct((count, 2 * vec, rows), BF16), jax.ShapeDtypeStruct((count * vec // places, vec), F32)]
    return call(split_kernel, (at, values, kept, came), [SMEM] + [VMEM] * 3, [VMEM] * 2, shapes, scratch=[pltpu.VMEM((count * vec, vec), F32)])


def offsets():
    order = [0]
    for step in range(1, REACH + 1):
        order.append(-step)
        if step < REACH:
            order.append(step)
    return order


def couple_kernel(at_ref, terms_ref, *refs):
    pieces, (total_ref, own_ref) = refs[:RING], refs[RING:]
    count, rows, vec = pieces[0].shape
    for piece, offset in zip(pieces, offsets()):
        place = (at_ref[2] + offset + RING) & (RING - 1)
        span = pl.ds(pl.multiple_of(place * rows, rows), rows)
        for k in range(count):
            own_ref[k, span] = piece[k]
    for k in range(count):
        both = jnp.dot(terms_ref[k], own_ref[k], preferred_element_type=F32)
        total_ref[k * vec : (k + 1) * vec] = both[:vec] + both[vec:]


def couple(at, terms, pieces):
    count, rows, vec = pieces[0].shape
    shapes = [jax.ShapeDtypeStruct((count * vec, vec), F32), jax.ShapeDtypeStruct((count, RING * rows, vec), BF16)]
    return call(couple_kernel, (at, terms, *pieces), [SMEM] + [VMEM] * (1 + RING), [VMEM, VMEM], shapes, 4 * count * RING * rows * vec * vec)


def spread_kernel(part_ref, below_ref, out_ref, token_ref):
    total = jnp.sum(part_ref[...], axis=0) / below_ref[...]
    for j in range(RING):
        out_ref[j] = total
    token_ref[...] = jnp.zeros_like(token_ref)


def spread(parts, below):
    return call(spread_kernel, (parts, below), [VMEM, VMEM], [VMEM] * 2, [jax.ShapeDtypeStruct((RING,) + parts.shape[1:], F32), TOKEN])


def scale_kernel(parts_ref, _, out_ref, token_ref):
    out_ref[...] = jnp.sum(parts_ref[...], axis=0).astype(BF16)
    token_ref[...] = jnp.zeros_like(token_ref)


def apply_kernel(at_ref, *refs):
    quarters, (scaled_ref, panels_ref, _, out_ref, block_ref, sems) = refs[:4], refs[4:]
    count, rows, _ = quarters[0].shape
    size = rows // RING
    copies = []
    for number, ref in enumerate(quarters):
        high = at_ref[1] if number < 2 else 1 - at_ref[1]
        core = at_ref[0] if number % 2 == 0 else 1 - at_ref[0]
        total = None
        for k in range(count):
            rotated = lax.dot_general(ref[k], scaled_ref[k], (((1,), (1,)), ((), ())), preferred_element_type=F32)
            term = lax.dot_general(rotated.astype(BF16), panels_ref[k], (((1,), (1,)), ((), ())), preferred_element_type=F32)
            total = term if total is None else total + term
        block_ref[number] = total.astype(BF16)
        for place in range(RING):
            target = pl.multiple_of((place * 4 + high * 2 + core) * size, size)
            source = block_ref.at[number, pl.ds(place * size, size)]
            copies.append(pltpu.make_async_copy(source, out_ref.at[pl.ds(target, size)], sems.at[len(copies)]))
            copies[-1].start()
    for copy in copies:
        copy.wait()


def apply(at, quarters, scaled, panels, token):
    count, rows, vec = quarters[0].shape
    width = panels.shape[1]
    return call(
        apply_kernel,
        (at, *quarters, scaled, panels, token),
        [SMEM] + [VMEM] * 6 + [ANY],
        ANY,
        jax.ShapeDtypeStruct((4 * rows, width), BF16),
        8 * count * rows * vec * (vec + width),
        [pltpu.VMEM((4, rows, width), BF16), pltpu.SemaphoreType.DMA((4 * RING,))],
        limit=24,
    )


def body(gradient, in_panels, out_pool, eigenvalues, owners):
    core, high, here = (lax.axis_index(a) for a in ("core", "yh", "z"))
    at = jnp.concatenate([jnp.stack([core, high, here, lax.axis_index(PLANE)]).astype(jnp.int32), owners])
    count, _, vec = in_panels.shape
    size = out_pool.shape[1] // (4 * RING)
    piece = jax.ShapeDtypeStruct((count, size, vec), BF16)

    with jax.named_scope("scatter"):
        every = lax.all_to_all(out_pool.reshape(2 * RING, 2 * size, vec), ("z", "yh"), 0, 0)

    with jax.named_scope("projection"):
        sent, _ = project(at, False, gradient, in_panels)
        kept, one = project(at, True, gradient, in_panels)
        kept, sent, two = pool(at, kept, [swap(x, "core") for x in sent])
        terms, below = split(at, eigenvalues, kept, swap(sent, "yh"), 32)

    with jax.named_scope("gather"):
        scratch = [pltpu.SemaphoreType.DMA((2 * count,))]
        specs = [SMEM, ANY, ANY, ANY]
        mine, send = call(pick_kernel, (at, every, one, two), specs, [VMEM] * 2, [piece] * 2, scratch=scratch)
        mine = level(at, mine, swap(send, "core"))
        pieces = [mine]
        up = down = mine
        for _ in range(1, REACH):
            up, down = shift(up, 1), shift(down, -1)
            pieces += [up, down]
        pieces.append(shift(up, 1))

    with jax.named_scope("coupling"):
        part, own = couple(at, terms, pieces)
        far = swap(own, "yh")
        part, token = spread(lax.all_to_all(part.reshape(32, -1, vec), PLANE, 0, 0), below)
        near, token = lax.optimization_barrier((own, token))
        near = swap(near, "core")
        part = lax.all_to_all(part, "z", 0, 0)
        shapes = [jax.ShapeDtypeStruct(part.shape[1:], BF16), TOKEN]
        scaled, token = call(scale_kernel, (part, token), [VMEM, ANY], [VMEM, VMEM], shapes)
        far, token = lax.optimization_barrier((far, token))
        quarters = [own, near, far, swap(far, "core")]
        copies = jnp.broadcast_to(scaled[None], (32,) + scaled.shape)
        scaled = lax.all_to_all(copies, PLANE, 0, 0).reshape(count, vec, vec)

    with jax.named_scope("output"):
        return apply(at, quarters, scaled, in_panels, token)


def solution(mesh):
    fine = Mesh(mesh.devices.reshape(2, 4, 2, 8, 2), ROW + COL)
    return jax.shard_map(
        body,
        mesh=fine,
        in_specs=(P(ROW, COL), P(None, COL, None), P(COL, ROW, None), P(), P()),
        out_specs=P(ROW, COL),
        check_vma=False,
    )
```

```python
import functools

import jax
import jax.numpy as jnp
from jax import lax
from jax.experimental import pallas as pl
from jax.experimental.pallas import tpu as pltpu
from jax.sharding import Mesh
from jax.sharding import PartitionSpec as P

ROW = ("yl", "x")
COL = ("yh", "z", "core")
PLANE = ("core", "yl", "x", "yh")
F32 = jnp.float32
BF16 = jnp.bfloat16
RING = 8
REACH = RING // 2
MIB = 1024 * 1024

VMEM = pl.BlockSpec(memory_space=pltpu.VMEM)
SMEM = pl.BlockSpec(memory_space=pltpu.SMEM)
ANY = pl.BlockSpec(memory_space=pl.ANY)
TOKEN = jax.ShapeDtypeStruct((8, 128), F32)


def swap(x, axis):
    return lax.ppermute(x, axis, [(0, 1), (1, 0)])


def shift(x, by):
    return lax.ppermute(x, "z", [(i, (i + by) % RING) for i in range(RING)])


def call(kernel, args, in_specs, out_specs, out_shape, flops=0, scratch=(), limit=16):
    moved = sum(a.size * a.dtype.itemsize for a in args)
    return pl.pallas_call(
        kernel,
        in_specs=in_specs,
        out_specs=out_specs,
        out_shape=out_shape,
        scratch_shapes=scratch,
        compiler_params=pltpu.CompilerParams(vmem_limit_bytes=limit * MIB),
        cost_estimate=pl.CostEstimate(flops=flops, bytes_accessed=moved, transcendentals=0),
    )(*args)


def owner_of(at_ref, k):
    number = at_ref[4 + k]
    return number & 1, (number >> 1) & (RING - 1), number >> 4


def pick_kernel(at_ref, all_ref, _one, _two, keep_ref, send_ref, sems):
    rows = keep_ref.shape[1]
    copies = []
    for k in range(keep_ref.shape[0]):
        _, place, high = owner_of(at_ref, k)
        for half, ref in ((at_ref[0], keep_ref), (1 - at_ref[0], send_ref)):
            span = pl.ds(pl.multiple_of(half * rows, rows), rows)
            copies.append(pltpu.make_async_copy(all_ref.at[place * 2 + high, span], ref.at[k], sems.at[len(copies)]))
            copies[-1].start()
    for copy in copies:
        copy.wait()


def level_kernel(at_ref, mine_ref, other_ref, out_ref):
    for k in range(out_ref.shape[0]):
        core, _, _ = owner_of(at_ref, k)

        @pl.when(core == at_ref[0])
        def _():
            out_ref[k] = mine_ref[k]

        @pl.when(core != at_ref[0])
        def _():
            out_ref[k] = other_ref[k]


def level(at, mine, other):
    return call(level_kernel, (at, mine, other), [SMEM, VMEM, VMEM], VMEM, jax.ShapeDtypeStruct(mine.shape, mine.dtype))


def project_kernel(own, at_ref, gradient_ref, panels_ref, *refs):
    outs, (token_ref, rows_ref, sems) = refs[:-3], refs[-3:]
    size = rows_ref.shape[0] // (2 * RING)
    half = at_ref[0] if own else 1 - at_ref[0]
    copies = []
    for high in range(2):
        for place in range(RING):
            start = pl.multiple_of((place * 4 + high * 2 + half) * size, size)
            target = rows_ref.at[pl.ds(len(copies) * size, size)]
            copies.append(pltpu.make_async_copy(gradient_ref.at[pl.ds(start, size)], target, sems.at[len(copies)]))
            copies[-1].start()
    for i in range(0, len(copies), 4):
        for copy in copies[i : i + 4]:
            copy.wait()
        span = slice(i * size, (i + 4) * size)
        for k, out_ref in enumerate(outs):
            out_ref[span] = jnp.dot(rows_ref[span], panels_ref[k], preferred_element_type=F32)
    token_ref[...] = jnp.zeros_like(token_ref)


def project(at, own, gradient, panels):
    count, width, vec = panels.shape
    rows = gradient.shape[0] // 2
    *outs, token = call(
        functools.partial(project_kernel, own),
        (at, gradient, panels),
        [SMEM, ANY, VMEM],
        [VMEM] * (count + 1),
        [jax.ShapeDtypeStruct((rows, vec), F32)] * count + [TOKEN],
        2 * rows * width * vec * count,
        [pltpu.VMEM((rows, width), BF16), pltpu.SemaphoreType.DMA((2 * RING,))],
    )
    return outs, token


def pool_kernel(count, at_ref, *refs):
    kept, came = refs[:count], refs[count : 2 * count]
    keep_ref, send_ref, token_ref = refs[2 * count :]
    rows = keep_ref.shape[1]
    mine = pl.ds(pl.multiple_of(at_ref[1] * rows, rows), rows)
    other = pl.ds(pl.multiple_of((1 - at_ref[1]) * rows, rows), rows)
    for k in range(count):
        keep_ref[k] = kept[k][mine] + came[k][mine]
        send_ref[k] = (kept[k][other] + came[k][other]).astype(BF16)
    token_ref[...] = jnp.zeros_like(token_ref)


def pool(at, kept, came):
    count = len(kept)
    rows, vec = kept[0].shape
    half = (count, rows // 2, vec)
    shapes = [jax.ShapeDtypeStruct(half, F32), jax.ShapeDtypeStruct(half, BF16), TOKEN]
    return call(functools.partial(pool_kernel, count), (at, *kept, *came), [SMEM] + [VMEM] * (2 * count), [VMEM] * 3, shapes)


def split_kernel(at_ref, values_ref, kept_ref, came_ref, out_ref, below_ref, all_ref):
    count, _, vec = kept_ref.shape
    for k in range(count):
        total = (kept_ref[k] + came_ref[k].astype(F32)).T
        high = total.astype(BF16)
        out_ref[k, :vec] = high
        out_ref[k, vec:] = (total - high.astype(F32)).astype(BF16)
        values = values_ref[k]
        all_ref[k * vec : (k + 1) * vec] = (values + 0.1 * jnp.mean(values)).T
    size = below_ref.shape[0]
    below_ref[...] = all_ref[pl.ds(pl.multiple_of(at_ref[3] * size, size), size)]


def split(at, values, kept, came, places):
    count, rows, vec = kept.shape
    shapes = [jax.ShapeDtypeStruct((count, 2 * vec, rows), BF16), jax.ShapeDtypeStruct((count * vec // places, vec), F32)]
    return call(split_kernel, (at, values, kept, came), [SMEM] + [VMEM] * 3, [VMEM] * 2, shapes, scratch=[pltpu.VMEM((count * vec, vec), F32)])


def offsets():
    order = [0]
    for step in range(1, REACH + 1):
        order.append(-step)
        if step < REACH:
            order.append(step)
    return order


def couple_kernel(at_ref, terms_ref, *refs):
    pieces, (total_ref, own_ref) = refs[:RING], refs[RING:]
    count, rows, vec = pieces[0].shape
    for piece, offset in zip(pieces, offsets()):
        place = (at_ref[2] + offset + RING) & (RING - 1)
        span = pl.ds(pl.multiple_of(place * rows, rows), rows)
        for k in range(count):
            own_ref[k, span] = piece[k]
    for k in range(count):
        both = jnp.dot(terms_ref[k], own_ref[k], preferred_element_type=F32)
        total_ref[k * vec : (k + 1) * vec] = both[:vec] + both[vec:]


def couple(at, terms, pieces):
    count, rows, vec = pieces[0].shape
    shapes = [jax.ShapeDtypeStruct((count * vec, vec), F32), jax.ShapeDtypeStruct((count, RING * rows, vec), BF16)]
    return call(couple_kernel, (at, terms, *pieces), [SMEM] + [VMEM] * (1 + RING), [VMEM, VMEM], shapes, 4 * count * RING * rows * vec * vec)


def spread_kernel(part_ref, below_ref, out_ref, token_ref):
    total = jnp.sum(part_ref[...], axis=0) / below_ref[...]
    for j in range(RING):
        out_ref[j] = total
    token_ref[...] = jnp.zeros_like(token_ref)


def spread(parts, below):
    return call(spread_kernel, (parts, below), [VMEM, VMEM], [VMEM] * 2, [jax.ShapeDtypeStruct((RING,) + parts.shape[1:], F32), TOKEN])


def scale_kernel(parts_ref, _, out_ref, token_ref):
    out_ref[...] = jnp.sum(parts_ref[...], axis=0).astype(BF16)
    token_ref[...] = jnp.zeros_like(token_ref)


def apply_kernel(at_ref, own_ref, last_ref, near_ref, far_ref, scaled_ref, panels_ref, _, out_ref, come_ref, block_ref, come_sems, sems):
    count, rows, _ = own_ref.shape
    size = rows // RING
    fetches = []
    for number, ref in enumerate((near_ref, far_ref)):
        fetches.append(pltpu.make_async_copy(ref, come_ref.at[number], come_sems.at[number]))
        fetches[-1].start()
    core, high = at_ref[0], at_ref[1]
    order = ((own_ref, high, core), (last_ref, 1 - high, 1 - core), (come_ref.at[0], high, 1 - core), (come_ref.at[1], 1 - high, core))
    copies = []
    for number, (ref, of_high, of_core) in enumerate(order):
        if number >= 2:
            fetches[number - 2].wait()
        total = None
        for k in range(count):
            rotated = lax.dot_general(ref[k], scaled_ref[k], (((1,), (1,)), ((), ())), preferred_element_type=F32)
            term = lax.dot_general(rotated.astype(BF16), panels_ref[k], (((1,), (1,)), ((), ())), preferred_element_type=F32)
            total = term if total is None else total + term
        block_ref[number] = total.astype(BF16)
        for place in range(RING):
            target = pl.multiple_of((place * 4 + of_high * 2 + of_core) * size, size)
            source = block_ref.at[number, pl.ds(place * size, size)]
            copies.append(pltpu.make_async_copy(source, out_ref.at[pl.ds(target, size)], sems.at[len(copies)]))
            copies[-1].start()
    for copy in copies:
        copy.wait()


def apply(at, own, last, near, far, scaled, panels, token):
    count, rows, vec = own.shape
    width = panels.shape[1]
    return call(
        apply_kernel,
        (at, own, last, near, far, scaled, panels, token),
        [SMEM, VMEM, VMEM, ANY, ANY, VMEM, VMEM, ANY],
        ANY,
        jax.ShapeDtypeStruct((4 * rows, width), BF16),
        8 * count * rows * vec * (vec + width),
        [
            pltpu.VMEM((2, count, rows, vec), BF16),
            pltpu.VMEM((4, rows, width), BF16),
            pltpu.SemaphoreType.DMA((2,)),
            pltpu.SemaphoreType.DMA((4 * RING,)),
        ],
        limit=24,
    )


def body(gradient, in_panels, out_pool, eigenvalues, owners):
    core, high, here = (lax.axis_index(a) for a in ("core", "yh", "z"))
    at = jnp.concatenate([jnp.stack([core, high, here, lax.axis_index(PLANE)]).astype(jnp.int32), owners])
    count, _, vec = in_panels.shape
    size = out_pool.shape[1] // (4 * RING)
    piece = jax.ShapeDtypeStruct((count, size, vec), BF16)

    with jax.named_scope("scatter"):
        every = lax.all_to_all(out_pool.reshape(2 * RING, 2 * size, vec), ("z", "yh"), 0, 0)

    with jax.named_scope("projection"):
        sent, _ = project(at, False, gradient, in_panels)
        kept, one = project(at, True, gradient, in_panels)
        kept, sent, two = pool(at, kept, [swap(x, "core") for x in sent])
        terms, below = split(at, eigenvalues, kept, swap(sent, "yh"), 32)

    with jax.named_scope("gather"):
        scratch = [pltpu.SemaphoreType.DMA((2 * count,))]
        specs = [SMEM, ANY, ANY, ANY]
        mine, send = call(pick_kernel, (at, every, one, two), specs, [VMEM] * 2, [piece] * 2, scratch=scratch)
        mine = level(at, mine, swap(send, "core"))
        pieces = [mine]
        up = down = mine
        for _ in range(1, REACH):
            up, down = shift(up, 1), shift(down, -1)
            pieces += [up, down]
        pieces.append(shift(up, 1))

    with jax.named_scope("coupling"):
        part, own = couple(at, terms, pieces)
        far = swap(own, "yh")
        part, token = spread(lax.all_to_all(part.reshape(32, -1, vec), PLANE, 0, 0), below)
        near, token = lax.optimization_barrier((own, token))
        near = swap(near, "core")
        part = lax.all_to_all(part, "z", 0, 0)
        shapes = [jax.ShapeDtypeStruct(part.shape[1:], BF16), TOKEN]
        scaled, token = call(scale_kernel, (part, token), [VMEM, ANY], [VMEM, VMEM], shapes)
        far, token = lax.optimization_barrier((far, token))
        last = swap(far, "core")
        copies = jnp.broadcast_to(scaled[None], (32,) + scaled.shape)
        scaled = lax.all_to_all(copies, PLANE, 0, 0).reshape(count, vec, vec)

    with jax.named_scope("output"):
        return apply(at, own, last, near, far, scaled, in_panels, token)


def solution(mesh):
    fine = Mesh(mesh.devices.reshape(2, 4, 2, 8, 2), ROW + COL)
    return jax.shard_map(
        body,
        mesh=fine,
        in_specs=(P(ROW, COL), P(None, COL, None), P(COL, ROW, None), P(), P()),
        out_specs=P(ROW, COL),
        check_vma=False,
    )
```

```python
import functools

import jax
import jax.numpy as jnp
from jax import lax
from jax.experimental import pallas as pl
from jax.experimental.pallas import tpu as pltpu
from jax.sharding import Mesh
from jax.sharding import PartitionSpec as P

ROW = ("yl", "x")
COL = ("yh", "z", "core")
PLANE = ("core", "yl", "x", "yh")
F32 = jnp.float32
BF16 = jnp.bfloat16
RING = 8
REACH = RING // 2
MIB = 1024 * 1024

VMEM = pl.BlockSpec(memory_space=pltpu.VMEM)
SMEM = pl.BlockSpec(memory_space=pltpu.SMEM)
ANY = pl.BlockSpec(memory_space=pl.ANY)
TOKEN = jax.ShapeDtypeStruct((8, 128), F32)


def swap(x, axis):
    return lax.ppermute(x, axis, [(0, 1), (1, 0)])


def shift(x, by):
    return lax.ppermute(x, "z", [(i, (i + by) % RING) for i in range(RING)])


def call(kernel, args, in_specs, out_specs, out_shape, flops=0, scratch=(), limit=16):
    moved = sum(a.size * a.dtype.itemsize for a in args)
    return pl.pallas_call(
        kernel,
        in_specs=in_specs,
        out_specs=out_specs,
        out_shape=out_shape,
        scratch_shapes=scratch,
        compiler_params=pltpu.CompilerParams(vmem_limit_bytes=limit * MIB),
        cost_estimate=pl.CostEstimate(flops=flops, bytes_accessed=moved, transcendentals=0),
    )(*args)


def owner_of(at_ref, k):
    number = at_ref[4 + k]
    return number & 1, (number >> 1) & (RING - 1), number >> 4


def pick_kernel(at_ref, all_ref, _one, _two, keep_ref, send_ref, sems):
    rows = keep_ref.shape[1]
    copies = []
    for k in range(keep_ref.shape[0]):
        _, place, high = owner_of(at_ref, k)
        for half, ref in ((at_ref[0], keep_ref), (1 - at_ref[0], send_ref)):
            span = pl.ds(pl.multiple_of(half * rows, rows), rows)
            copies.append(pltpu.make_async_copy(all_ref.at[place * 2 + high, span], ref.at[k], sems.at[len(copies)]))
            copies[-1].start()
    for copy in copies:
        copy.wait()


def level_kernel(at_ref, mine_ref, other_ref, out_ref):
    for k in range(out_ref.shape[0]):
        core, _, _ = owner_of(at_ref, k)

        @pl.when(core == at_ref[0])
        def _():
            out_ref[k] = mine_ref[k]

        @pl.when(core != at_ref[0])
        def _():
            out_ref[k] = other_ref[k]


def level(at, mine, other):
    return call(level_kernel, (at, mine, other), [SMEM, VMEM, VMEM], VMEM, jax.ShapeDtypeStruct(mine.shape, mine.dtype))


def project_kernel(own, at_ref, gradient_ref, panels_ref, *refs):
    outs, (token_ref, rows_ref, sems) = refs[:-3], refs[-3:]
    size = rows_ref.shape[0] // (2 * RING)
    half = at_ref[0] if own else 1 - at_ref[0]
    copies = []
    for high in range(2):
        for place in range(RING):
            start = pl.multiple_of((place * 4 + high * 2 + half) * size, size)
            target = rows_ref.at[pl.ds(len(copies) * size, size)]
            copies.append(pltpu.make_async_copy(gradient_ref.at[pl.ds(start, size)], target, sems.at[len(copies)]))
            copies[-1].start()
    for i in range(0, len(copies), 4):
        for copy in copies[i : i + 4]:
            copy.wait()
        span = slice(i * size, (i + 4) * size)
        for k, out_ref in enumerate(outs):
            out_ref[span] = jnp.dot(rows_ref[span], panels_ref[k], preferred_element_type=F32)
    token_ref[...] = jnp.zeros_like(token_ref)


def project(at, own, gradient, panels):
    count, width, vec = panels.shape
    rows = gradient.shape[0] // 2
    *outs, token = call(
        functools.partial(project_kernel, own),
        (at, gradient, panels),
        [SMEM, ANY, VMEM],
        [VMEM] * (count + 1),
        [jax.ShapeDtypeStruct((rows, vec), F32)] * count + [TOKEN],
        2 * rows * width * vec * count,
        [pltpu.VMEM((rows, width), BF16), pltpu.SemaphoreType.DMA((2 * RING,))],
    )
    return outs, token


def pool_kernel(count, at_ref, *refs):
    kept, came = refs[:count], refs[count : 2 * count]
    keep_ref, send_ref, token_ref = refs[2 * count :]
    rows = keep_ref.shape[1]
    mine = pl.ds(pl.multiple_of(at_ref[1] * rows, rows), rows)
    other = pl.ds(pl.multiple_of((1 - at_ref[1]) * rows, rows), rows)
    for k in range(count):
        keep_ref[k] = kept[k][mine] + came[k][mine]
        send_ref[k] = (kept[k][other] + came[k][other]).astype(BF16)
    token_ref[...] = jnp.zeros_like(token_ref)


def pool(at, kept, came):
    count = len(kept)
    rows, vec = kept[0].shape
    half = (count, rows // 2, vec)
    shapes = [jax.ShapeDtypeStruct(half, F32), jax.ShapeDtypeStruct(half, BF16), TOKEN]
    return call(functools.partial(pool_kernel, count), (at, *kept, *came), [SMEM] + [VMEM] * (2 * count), [VMEM] * 3, shapes)


def split_kernel(at_ref, values_ref, kept_ref, came_ref, out_ref, below_ref, all_ref):
    count, _, vec = kept_ref.shape
    for k in range(count):
        total = (kept_ref[k] + came_ref[k].astype(F32)).T
        high = total.astype(BF16)
        out_ref[k, :vec] = high
        out_ref[k, vec:] = (total - high.astype(F32)).astype(BF16)
        values = values_ref[k]
        all_ref[k * vec : (k + 1) * vec] = (values + 0.1 * jnp.mean(values)).T
    size = below_ref.shape[0]
    below_ref[...] = all_ref[pl.ds(pl.multiple_of(at_ref[3] * size, size), size)]


def split(at, values, kept, came, places):
    count, rows, vec = kept.shape
    shapes = [jax.ShapeDtypeStruct((count, 2 * vec, rows), BF16), jax.ShapeDtypeStruct((count * vec // places, vec), F32)]
    return call(split_kernel, (at, values, kept, came), [SMEM] + [VMEM] * 3, [VMEM] * 2, shapes, scratch=[pltpu.VMEM((count * vec, vec), F32)])


def offsets():
    order = [0]
    for step in range(1, REACH + 1):
        order.append(-step)
        if step < REACH:
            order.append(step)
    return order


def couple_kernel(at_ref, terms_ref, *refs):
    pieces, (total_ref, own_ref) = refs[:RING], refs[RING:]
    count, rows, vec = pieces[0].shape
    for piece, offset in zip(pieces, offsets()):
        place = (at_ref[2] + offset + RING) & (RING - 1)
        span = pl.ds(pl.multiple_of(place * rows, rows), rows)
        for k in range(count):
            own_ref[k, span] = piece[k]
    for k in range(count):
        both = jnp.dot(terms_ref[k], own_ref[k], preferred_element_type=F32)
        total_ref[k * vec : (k + 1) * vec] = both[:vec] + both[vec:]


def couple(at, terms, pieces):
    count, rows, vec = pieces[0].shape
    shapes = [jax.ShapeDtypeStruct((count * vec, vec), F32), jax.ShapeDtypeStruct((count, RING * rows, vec), BF16)]
    return call(couple_kernel, (at, terms, *pieces), [SMEM] + [VMEM] * (1 + RING), [VMEM, VMEM], shapes, 4 * count * RING * rows * vec * vec)


def spread_kernel(part_ref, below_ref, out_ref, token_ref):
    total = jnp.sum(part_ref[...], axis=0) / below_ref[...]
    for j in range(RING):
        out_ref[j] = total
    token_ref[...] = jnp.zeros_like(token_ref)


def spread(parts, below):
    return call(spread_kernel, (parts, below), [VMEM, VMEM], [VMEM] * 2, [jax.ShapeDtypeStruct((RING,) + parts.shape[1:], F32), TOKEN])


def scale_kernel(parts_ref, _, out_ref):
    out_ref[...] = jnp.sum(parts_ref[...], axis=0).astype(BF16)


def apply_kernel(near, at_ref, own_ref, other_ref, scaled_ref, panels_ref, _, out_ref, block_ref, sems):
    count, rows, _ = own_ref.shape
    size = rows // RING
    high = at_ref[1] if near else 1 - at_ref[1]
    copies = []
    total = None
    for k in range(count):
        parts = [lax.dot_general(ref[k], scaled_ref[k], (((1,), (1,)), ((), ())), preferred_element_type=F32) for ref in (own_ref, other_ref)]
        rotated = jnp.concatenate(parts, axis=0).astype(BF16)
        term = lax.dot_general(rotated, panels_ref[k], (((1,), (1,)), ((), ())), preferred_element_type=F32)
        total = term if total is None else total + term
    for number, core in enumerate((at_ref[0], 1 - at_ref[0])):
        block_ref[number] = total[number * rows : (number + 1) * rows].astype(BF16)
        for place in range(RING):
            target = pl.multiple_of((place * 4 + high * 2 + core) * size, size)
            source = block_ref.at[number, pl.ds(place * size, size)]
            copies.append(pltpu.make_async_copy(source, out_ref.at[pl.ds(target, size)], sems.at[len(copies)]))
            copies[-1].start()
    for copy in copies:
        copy.wait()


def apply(near, at, own, other, scaled, panels, into):
    count, rows, vec = own.shape
    width = panels.shape[1]
    return pl.pallas_call(
        functools.partial(apply_kernel, near),
        in_specs=[SMEM, VMEM, VMEM, VMEM, VMEM, ANY],
        out_specs=ANY,
        out_shape=jax.ShapeDtypeStruct((4 * rows, width), BF16),
        input_output_aliases={} if near else {5: 0},
        scratch_shapes=[pltpu.VMEM((2, rows, width), BF16), pltpu.SemaphoreType.DMA((2 * RING,))],
        compiler_params=pltpu.CompilerParams(vmem_limit_bytes=24 * MIB),
        cost_estimate=pl.CostEstimate(flops=4 * count * rows * vec * (vec + width), bytes_accessed=4 * rows * width, transcendentals=0),
    )(at, own, other, scaled, panels, into)


def body(gradient, in_panels, out_pool, eigenvalues, owners):
    core, high, here = (lax.axis_index(a) for a in ("core", "yh", "z"))
    at = jnp.concatenate([jnp.stack([core, high, here, lax.axis_index(PLANE)]).astype(jnp.int32), owners])
    count, _, vec = in_panels.shape
    size = out_pool.shape[1] // (4 * RING)
    piece = jax.ShapeDtypeStruct((count, size, vec), BF16)

    with jax.named_scope("scatter"):
        every = lax.all_to_all(out_pool.reshape(2 * RING, 2 * size, vec), ("z", "yh"), 0, 0)

    with jax.named_scope("projection"):
        sent, _ = project(at, False, gradient, in_panels)
        kept, one = project(at, True, gradient, in_panels)
        kept, sent, two = pool(at, kept, [swap(x, "core") for x in sent])
        terms, below = split(at, eigenvalues, kept, swap(sent, "yh"), 32)

    with jax.named_scope("gather"):
        scratch = [pltpu.SemaphoreType.DMA((2 * count,))]
        specs = [SMEM, ANY, ANY, ANY]
        mine, send = call(pick_kernel, (at, every, one, two), specs, [VMEM] * 2, [piece] * 2, scratch=scratch)
        mine = level(at, mine, swap(send, "core"))
        pieces = [mine]
        up = down = mine
        for _ in range(1, REACH):
            up, down = shift(up, 1), shift(down, -1)
            pieces += [up, down]
        pieces.append(shift(up, 1))

    with jax.named_scope("coupling"):
        part, own = couple(at, terms, pieces)
        part, token = spread(lax.all_to_all(part.reshape(32, -1, vec), PLANE, 0, 0), below)
        own, token = lax.optimization_barrier((own, token))
        far, other = swap(own, "yh"), swap(own, "core")
        part = lax.all_to_all(part, "z", 0, 0)
        scaled = call(scale_kernel, (part, token), [VMEM, ANY], VMEM, jax.ShapeDtypeStruct(part.shape[1:], BF16))
        copies = jnp.broadcast_to(scaled[None], (32,) + scaled.shape)
        scaled = lax.all_to_all(copies, PLANE, 0, 0).reshape(count, vec, vec)

    with jax.named_scope("output"):
        far, token = lax.optimization_barrier((far, scaled[0, :16, :128]))
        out = apply(True, at, own, other, scaled, in_panels, token)
        return apply(False, at, far, swap(far, "core"), scaled, in_panels, out)


def solution(mesh):
    fine = Mesh(mesh.devices.reshape(2, 4, 2, 8, 2), ROW + COL)
    return jax.shard_map(
        body,
        mesh=fine,
        in_specs=(P(ROW, COL), P(None, COL, None), P(COL, ROW, None), P(), P()),
        out_specs=P(ROW, COL),
        check_vma=False,
    )
```
